32 devices in a mesh: rep: 8 (over z, core), fsdp: 4 (over y, x).
Axes of the slice: x: 2, y: 2, z: 4, core: 2. Of those that a mesh axis runs over, the one named last changes fastest.
Arguments:
- hidden: bfloat16 [8, 768, 8192], P('rep', 'fsdp'), may hold values from -6 to 6
- key_cotangent: bfloat16 [8, 768, 1024], P('rep', 'fsdp'), may hold values from -6 to 6
- local_weight: float32 [8, 8192, 1024], P('rep', 'fsdp'), may hold values from -6 to 6
- adam_first: float32 [8, 8192, 1024], P('rep', 'fsdp'), may hold values from -2 to 2
- adam_second: float32 [8, 8192, 1024], P('rep', 'fsdp'), may hold values from 0.02 to 0.3
- outer_weight: float32 [4, 2048, 1024], P('fsdp', 'rep'), may hold values from -6 to 6
- outer_momentum: float32 [4, 2048, 1024], P('fsdp', 'rep'), may hold values from -2 to 2
- roster: int32 [8, 4], replicated, may hold values from 0 to 3, each once within a row
- step_count: int32 [1], replicated, may hold values from 0 to 31
Outputs:
- projected_keys: bfloat16 [8, 768, 1024], P('rep', 'fsdp')
- input_grad: bfloat16 [8, 768, 8192], P('rep', 'fsdp')
- new_local: float32 [8, 8192, 1024], P('rep', 'fsdp')
- new_outer: float32 [4, 2048, 1024], P('fsdp', 'rep')
- new_momentum: float32 [4, 2048, 1024], P('fsdp', 'rep')
The draws below stay inside these ranges and needn't reach their ends.
Inputs may be any that keep to these rules, and one draw needn't show every extreme that they name: `roster`: each row names every fragment index once.
All inputs are finite; a program needn't handle non-finite values.
Results may differ from the reference program's by a relative error of at most 0.0045.
The reference program's roundings to bfloat16 on the way count: a program that leaves them out, or rounds other values in their place, can miss the bound.
Values may be sent and summed in bfloat16 or wider, within the bound.
No kernel may reach another device: no remote copies, remote signals or barrier semaphores. Data moves between devices by JAX's collectives and lax.ppermute only.
A program may use at most 192 MiB of HBM per device.

```python
import math
import jax
import jax.numpy as jnp
from jax import lax

D = 8192
TOK_DEV = 192
FRAGS = 4
ROUNDS = 8
KEYS = 1024
FRAG_COLS = 256
REPLICAS = 8
SHARDS = 4
BLOCK = 2048
TOK_REP = 768
N_REP = 8
N_FSDP = 4


def steps_of(stream_key, dims, cuts, smallest, largest):
    def one(axis_at, blocks):
        heights = jax.random.uniform(jax.random.fold_in(jax.random.fold_in(stream_key, 6), axis_at), (blocks,), jnp.float32, smallest / len(cuts), largest / len(cuts))
        return jnp.repeat(jnp.exp(heights), dims[axis_at] // blocks).reshape((-1,) + (1,) * (len(dims) - axis_at - 1))

    factor_of = one(*cuts[0])
    for cut in cuts[1:]:
        factor_of = factor_of * one(*cut)
    return factor_of


def scatter_about(rng, extent, deviation, limit, split=(), held_as=jnp.bfloat16):
    entries = jax.random.normal(rng, extent, jnp.float32) * deviation
    if len(split) > 0:
        entries = steps_of(rng, extent, split, -0.22, 0.18) * entries
    return jnp.clip(entries, min=-limit, max=limit).astype(held_as)


def setup_inputs(seed: int = 0) -> dict:
    key_of = jax.random.split(jax.random.key(seed), 10)
    hidden = scatter_about(key_of[0], (REPLICAS, TOK_REP, D), 1.0, 6.0, ((0, 8), (1, 4)))
    key_cotangent = scatter_about(key_of[1], (REPLICAS, TOK_REP, KEYS), 1.0, 6.0, ((0, 8), (1, 4)))
    local_weight = scatter_about(key_of[2], (REPLICAS, D, KEYS), 1.0, 6.0, ((0, 8), (1, 4)), jnp.float32)
    adam_first = scatter_about(key_of[3], (REPLICAS, D, KEYS), 0.3, 2.0, ((0, 8), (1, 4)), jnp.float32)
    adam_second = jnp.clip(jnp.exp(math.log(0.3) - 2.7080503 * jax.random.uniform(key_of[4], (REPLICAS, D, KEYS), jnp.float32) ** steps_of(key_of[4], (REPLICAS, D, KEYS), ((0, 8), (1, 4)), -0.2, 0.2)), 0.02, 0.3)
    outer_weight = scatter_about(key_of[5], (SHARDS, BLOCK, KEYS), 1.0, 6.0, ((0, 4), (1, 8)), jnp.float32)
    outer_momentum = scatter_about(key_of[6], (SHARDS, BLOCK, KEYS), 0.3, 2.0, ((0, 4), (1, 8)), jnp.float32)
    roster = jax.vmap(lambda own: jax.random.permutation(own, FRAGS))(jax.random.split(key_of[7], ROUNDS)).reshape((ROUNDS, FRAGS)).astype(jnp.int32)
    step_count = jax.random.randint(key_of[8], (1,), 0, FRAGS * ROUNDS).astype(jnp.int32)
    return dict(hidden=hidden, key_cotangent=key_cotangent, local_weight=local_weight, adam_first=adam_first, adam_second=adam_second, outer_weight=outer_weight, outer_momentum=outer_momentum, roster=roster, step_count=step_count)


def adam_update(weight, first, second, grad, steps_done):
    first_new = 0.9 * first + 0.1 * grad
    second_new = 0.95 * second + 0.05 * grad * grad
    first_hat = first_new / (1.0 - jnp.power(jnp.float32(0.9), steps_done))
    second_hat = second_new / (1.0 - jnp.power(jnp.float32(0.95), steps_done))
    return weight - 0.1 * (first_hat / (jnp.sqrt(second_hat) + 1e-08) + 0.1 * weight)

def reference(hidden, key_cotangent, local_weight, adam_first, adam_second, outer_weight, outer_momentum, roster, step_count):
    factor = 1.0 / math.sqrt(D)
    fragment = roster[step_count[0] // FRAGS % ROUNDS, step_count[0] % FRAGS]
    column = (fragment * FRAG_COLS).astype(jnp.int32)
    steps_done = (step_count[0] + 1).astype(jnp.float32)

    def replica(items):
        tokens, cotangent, weight, first, second = items
        weight_half = weight.astype(jnp.bfloat16)
        keys_out = (jnp.dot(tokens, weight_half, preferred_element_type=jnp.float32) * factor).astype(jnp.bfloat16)
        back_out = (jnp.dot(cotangent, weight_half.T, preferred_element_type=jnp.float32) * factor).astype(jnp.bfloat16)
        token_groups = tokens.reshape(N_FSDP, TOK_DEV, D).astype(jnp.float32)
        cot_groups = cotangent.reshape(N_FSDP, TOK_DEV, KEYS).astype(jnp.float32)
        parts = (jnp.einsum('std,stk->sdk', token_groups, cot_groups) * factor).astype(jnp.bfloat16)
        parts = lax.optimization_barrier(parts)
        grad = lax.optimization_barrier(jnp.sum(parts.astype(jnp.float32), axis=0))
        inner = adam_update(weight, first, second, grad, steps_done)
        return (keys_out, back_out, inner)
    keys_all, back_all, inner_all = lax.map(replica, (hidden, key_cotangent, local_weight, adam_first, adam_second))
    outer_flat = outer_weight.reshape(D, KEYS)
    moment_flat = outer_momentum.reshape(D, KEYS)
    outer_frag = lax.dynamic_slice_in_dim(outer_flat, column, FRAG_COLS, 1)
    moment_frag = lax.dynamic_slice_in_dim(moment_flat, column, FRAG_COLS, 1)
    total = lax.optimization_barrier(jnp.sum(lax.dynamic_slice_in_dim(inner_all, column, FRAG_COLS, 2), axis=0))
    pseudo = outer_frag - total / N_REP
    moment_new = 0.9 * moment_frag + pseudo
    outer_new = outer_frag - 0.7 * (pseudo + 0.9 * moment_new)
    new_outer = lax.dynamic_update_slice_in_dim(outer_flat, outer_new, column, 1).reshape(N_FSDP, D // N_FSDP, KEYS)
    new_momentum = lax.dynamic_update_slice_in_dim(moment_flat, moment_new, column, 1).reshape(N_FSDP, D // N_FSDP, KEYS)
    spread = jnp.broadcast_to(outer_new[None], (N_REP, D, FRAG_COLS))
    new_local = lax.dynamic_update_slice_in_dim(inner_all, spread, column, 2)
    return (keys_all, back_all, new_local, new_outer, new_momentum)
```

```python
import functools
import math

import jax
import jax.numpy as jnp
from jax import lax
from jax.experimental import pallas as pl
from jax.experimental.pallas import tpu as pltpu
from jax.sharding import PartitionSpec as P

FRAGS = 4
ROUNDS = 8


def pair(x, axis, offset):
    size = lax.axis_size(axis)
    return lax.ppermute(x, axis, [(i, i ^ offset) for i in range(size)])


def adam_tile(groups, factor, scal_ref, hid_refs, cot_refs, weight_ref, first_ref, second_ref):
    grad = None
    for g in range(groups):
        part = lax.dot_general(
            hid_refs[g][...], cot_refs[g][...], (((0,), (0,)), ((), ())),
            preferred_element_type=jnp.float32,
        )
        part = (part * factor).astype(jnp.bfloat16).astype(jnp.float32)
        grad = part if grad is None else grad + part
    weight = weight_ref[...]
    first = 0.9 * first_ref[...] + 0.1 * grad
    second = 0.95 * second_ref[...] + 0.05 * grad * grad
    step = (first * scal_ref[0]) / (jnp.sqrt(second * scal_ref[1]) + 1e-08)
    return weight - 0.1 * (step + 0.1 * weight)


def adam_kernel(groups, factor, where_ref, scal_ref, *refs):
    hid_refs, cot_refs = refs[:groups], refs[groups : 2 * groups]
    weight_ref, first_ref, second_ref, out_ref = refs[2 * groups :]
    out_ref[...] = adam_tile(
        groups, factor, scal_ref, hid_refs, cot_refs, weight_ref, first_ref, second_ref
    ).astype(out_ref.dtype)


def adam_call(tokens, hid_peers, cots, weight, first, second, where, scal, factor, cols, by_frag, dtype, tile):
    rows, keys = weight.shape
    toks = tokens.shape[0]
    groups = len(cots)
    steps = rows // tile

    def col(w):
        return w[1] if by_frag else 0

    own = pl.BlockSpec((toks, tile), lambda i, w: (0, w[0] * steps + i))
    peer = pl.BlockSpec((toks, tile), lambda i, w: (0, i))
    cot = pl.BlockSpec((toks, cols), lambda i, w: (0, col(w)))
    state = pl.BlockSpec((tile, cols), lambda i, w: (i, col(w)))
    return pl.pallas_call(
        functools.partial(adam_kernel, groups, factor),
        grid_spec=pltpu.PrefetchScalarGridSpec(
            num_scalar_prefetch=1,
            grid=(steps,),
            in_specs=[pl.BlockSpec(memory_space=pltpu.SMEM), own]
            + [peer] * (groups - 1)
            + [cot] * groups
            + [state] * 3,
            out_specs=pl.BlockSpec((tile, cols), lambda i, w: (i, 0)),
        ),
        out_shape=jax.ShapeDtypeStruct((rows, cols), dtype),
        compiler_params=pltpu.CompilerParams(vmem_limit_bytes=32 * 1024 * 1024),
        cost_estimate=pl.CostEstimate(
            flops=2 * rows * cols * toks * groups,
            bytes_accessed=rows * cols * 16,
            transcendentals=2 * rows * cols,
        ),
    )(where, scal, tokens, *hid_peers, *cots, weight, first, second)


def per_device(
    hidden,
    key_cotangent,
    local_weight,
    adam_first,
    adam_second,
    outer_weight,
    outer_momentum,
    roster,
    step_count,
):
    tokens = hidden[0]
    cotangent = key_cotangent[0]
    weight = local_weight[0]
    outer_now = outer_weight[0]
    moment_now = outer_momentum[0]
    toks, width = tokens.shape
    rows, keys = weight.shape
    factor = 1.0 / math.sqrt(width)
    frag_cols = keys // FRAGS
    shards = lax.axis_size("fsdp")
    replicas = lax.axis_size("rep")
    shard = lax.axis_index("fsdp")
    replica = lax.axis_index("rep")
    offsets = list(range(1, shards))

    fragment = roster[step_count[0] // FRAGS % ROUNDS, step_count[0] % FRAGS]
    column = fragment * frag_cols
    steps_done = (step_count[0] + 1).astype(jnp.float32)
    scal = jnp.stack(
        [
            1.0 / (1.0 - jnp.power(jnp.float32(0.9), steps_done)),
            1.0 / (1.0 - jnp.power(jnp.float32(0.95), steps_done)),
        ]
    )
    where = jnp.stack([shard, fragment]).astype(jnp.int32)

    cots = [cotangent] + [pair(cotangent, "fsdp", m) for m in offsets]
    hid_peers = [
        pair(lax.dynamic_slice_in_dim(tokens, (shard ^ m) * rows, rows, 1), "fsdp", m)
        for m in offsets
    ]
    hid_own = lax.dynamic_slice_in_dim(tokens, shard * rows, rows, 1)

    weight_half = weight.astype(jnp.bfloat16)

    def back(cot):
        out = lax.dot_general(
            cot, weight_half, (((1,), (1,)), ((), ())), preferred_element_type=jnp.float32
        )
        return (out * factor).astype(jnp.bfloat16)

    def forward(hid):
        return jnp.dot(hid, weight_half, preferred_element_type=jnp.float32)

    back_blocks = [back(cotangent)] + [pair(back(cots[m]), "fsdp", m) for m in offsets]

    inner_frag = adam_call(
        tokens, hid_peers, cots, weight, adam_first[0], adam_second[0], where, scal, factor,
        frag_cols, True, jnp.bfloat16, 256,
    )
    chips = replicas // 2
    core, chip = replica % 2, replica // 2
    own_rows = rows // replicas
    blocks = inner_frag.reshape(chips, 2, own_rows, frag_cols)
    keep = lax.dynamic_index_in_dim(blocks, core, 1, keepdims=False)
    give = lax.dynamic_index_in_dim(blocks, 1 - core, 1, keepdims=False)
    pair_sum = keep.astype(jnp.float32) + pair(give, "rep", 1).astype(jnp.float32)
    pair_half = pair_sum.astype(jnp.bfloat16)
    total = lax.dynamic_index_in_dim(pair_sum, chip, 0, keepdims=False)
    for k in range(1, chips):
        block = lax.dynamic_index_in_dim(pair_half, chip ^ k, 0, keepdims=False)
        total = total + pair(block, "rep", 2 * k).astype(jnp.float32)
    outer_frag = lax.dynamic_slice_in_dim(outer_now, column, frag_cols, 1)
    moment_frag = lax.dynamic_slice_in_dim(moment_now, column, frag_cols, 1)
    pseudo = outer_frag - total / replicas
    moment_own = 0.9 * moment_frag + pseudo
    outer_own = outer_frag - 0.7 * (pseudo + 0.9 * moment_own)
    outer_half = outer_own.astype(jnp.bfloat16)
    same_core = jnp.zeros((chips, own_rows, frag_cols), jnp.bfloat16)
    same_core = lax.dynamic_update_index_in_dim(same_core, outer_half, chip, 0)
    for k in range(1, chips):
        same_core = lax.dynamic_update_index_in_dim(
            same_core, pair(outer_half, "rep", 2 * k), chip ^ k, 0
        )
    other_core = pair(same_core, "rep", 1)
    low = jnp.where(core == 0, same_core, other_core)
    high = jnp.where(core == 0, other_core, same_core)
    outer_back = jnp.stack([low, high], axis=1).reshape(rows, frag_cols).astype(jnp.float32)

    inner = adam_call(
        tokens, hid_peers, cots, weight, adam_first[0], adam_second[0], where, scal, factor,
        keys, False, jnp.float32, 256,
    )
    new_local = lax.dynamic_update_slice_in_dim(inner, outer_back, column, 1)

    key_acc = forward(hid_own)
    for m in offsets:
        part = forward(hid_peers[m - 1]).astype(jnp.bfloat16)
        key_acc = key_acc + pair(part, "fsdp", m).astype(jnp.float32)
    keys_out = (key_acc * factor).astype(jnp.bfloat16)

    back_out = jnp.zeros((toks, width), jnp.bfloat16)
    for m in range(shards):
        back_out = lax.dynamic_update_slice_in_dim(back_out, back_blocks[m], (shard ^ m) * rows, 1)

    outer_next = lax.dynamic_update_slice_in_dim(outer_now, outer_own, column, 1)
    moment_next = lax.dynamic_update_slice_in_dim(moment_now, moment_own, column, 1)
    return (keys_out[None], back_out[None], new_local[None], outer_next[None], moment_next[None])


def solution(mesh):
    in_specs = (
        P("rep", "fsdp", None),
        P("rep", "fsdp", None),
        P("rep", "fsdp", None),
        P("rep", "fsdp", None),
        P("rep", "fsdp", None),
        P("fsdp", "rep", None),
        P("fsdp", "rep", None),
        P(),
        P(),
    )
    out_specs = (
        P("rep", "fsdp", None),
        P("rep", "fsdp", None),
        P("rep", "fsdp", None),
        P("fsdp", "rep", None),
        P("fsdp", "rep", None),
    )
    return jax.shard_map(
        per_device, mesh=mesh, in_specs=in_specs, out_specs=out_specs, check_vma=False
    )
```

```python
import functools
import math

import jax
import jax.numpy as jnp
from jax import lax
from jax.experimental import pallas as pl
from jax.experimental.pallas import tpu as pltpu
from jax.sharding import PartitionSpec as P

FRAGS = 4
ROUNDS = 8
MIB = 1024 * 1024
VMEM = 48 * MIB
SMALL = pl.CostEstimate(flops=1, bytes_accessed=1, transcendentals=0)


def pair(x, axis, offset):
    size = lax.axis_size(axis)
    return lax.ppermute(x, axis, [(i, i ^ offset) for i in range(size)])


def after(x, *others):
    return lax.optimization_barrier((x, *others))[0]


def row_dot(hid, cot, factor):
    part = lax.dot_general(
        hid, cot, (((0,), (0,)), ((), ())), preferred_element_type=jnp.float32
    )
    return (part * factor).astype(jnp.bfloat16).astype(jnp.float32)


def dot_keys(hid, weight):
    return jnp.dot(hid, weight, preferred_element_type=jnp.float32)


def dot_back(cot, weight, factor):
    out = lax.dot_general(
        cot, weight, (((1,), (1,)), ((), ())), preferred_element_type=jnp.float32
    )
    return (out * factor).astype(jnp.bfloat16)


def add_keys(ref, value):
    @pl.when(pl.program_id(0) == 0)
    def _():
        ref[...] = value

    @pl.when(pl.program_id(0) > 0)
    def _():
        ref[...] += value


def own_kernel(factor, where_ref, tokens_ref, cot_ref, weight_ref, half_ref, back_ref, keys_ref, frag_ref):
    cols = frag_ref.shape[1]
    frag_ref[...] = weight_ref[:, pl.ds(pl.multiple_of(where_ref[1] * cols, cols), cols)]
    half = weight_ref[...].astype(jnp.bfloat16)
    half_ref[...] = half
    back_ref[...] = dot_back(cot_ref[...], half, factor)
    add_keys(keys_ref, dot_keys(tokens_ref[...], half))


def own_call(tokens, cot, weight, where, factor, tile, frag_cols):
    rows, keys = weight.shape
    toks, width = tokens.shape
    steps = rows // tile
    here = pl.BlockSpec((toks, tile), lambda i, w: (0, w[0] * steps + i))
    block = pl.BlockSpec((tile, keys), lambda i, w: (i, 0))
    whole = pl.BlockSpec((toks, keys), lambda i, w: (0, 0))
    return pl.pallas_call(
        functools.partial(own_kernel, factor),
        grid_spec=pltpu.PrefetchScalarGridSpec(
            num_scalar_prefetch=1,
            grid=(steps,),
            in_specs=[here, whole, block],
            out_specs=[block, here, whole, pl.BlockSpec((tile, frag_cols), lambda i, w: (i, 0))],
        ),
        out_shape=[
            jax.ShapeDtypeStruct((rows, keys), jnp.bfloat16),
            jax.ShapeDtypeStruct((toks, width), jnp.bfloat16),
            jax.ShapeDtypeStruct((toks, keys), jnp.float32),
            jax.ShapeDtypeStruct((rows, frag_cols), jnp.float32),
        ],
        compiler_params=pltpu.CompilerParams(vmem_limit_bytes=VMEM),
        cost_estimate=SMALL,
    )(where, tokens, cot, weight)


def cut_kernel(count, where_ref, *refs):
    for i in range(count):
        refs[count + i][...] = refs[i][...]


def cut_call(where, arrays, cols):
    count = len(arrays)
    rows = arrays[0].shape[0]
    return pl.pallas_call(
        functools.partial(cut_kernel, count),
        grid_spec=pltpu.PrefetchScalarGridSpec(
            num_scalar_prefetch=1,
            grid=(2,),
            in_specs=[pl.BlockSpec((rows // 2, cols), lambda i, w: (i, w[1]))] * count,
            out_specs=[pl.BlockSpec((rows // 2, cols), lambda i, w: (i, 0))] * count,
        ),
        out_shape=[jax.ShapeDtypeStruct((rows, cols), x.dtype) for x in arrays],
        compiler_params=pltpu.CompilerParams(vmem_limit_bytes=VMEM),
        cost_estimate=SMALL,
    )(where, *arrays)


def pack(outs, accs, hids, cots, weight, factor, step, steps):
    toks = hids[0].shape[0]
    tile = weight.shape[0]
    rows = tile * steps
    at = pl.ds(pl.multiple_of(step * tile, tile), tile)
    back = dot_back(jnp.concatenate(cots, axis=0), weight, factor)
    part = dot_keys(jnp.concatenate(hids, axis=0), weight)
    for g, (out, acc) in enumerate(zip(outs, accs)):
        mine = slice(g * toks, (g + 1) * toks)
        out[:, at] = back[mine]
        add_keys(acc, part[mine])

    @pl.when(step == steps - 1)
    def _():
        for out, acc in zip(outs, accs):
            out[:, rows:] = acc[...].astype(out.dtype)


def near_kernel(groups, factor, steps, where_ref, *refs):
    hids, cots, weight_ref = refs[:groups], refs[groups : 2 * groups], refs[2 * groups]
    all_ref, frag_ref, *outs = refs[2 * groups + 1 :]
    total = row_dot(hids[0][...], cots[0][...], factor)
    for g in range(1, groups):
        total = total + row_dot(hids[g][...], cots[g][...], factor)
    all_ref[...] = total
    cols = frag_ref.shape[1]
    frag_ref[...] = all_ref[:, pl.ds(pl.multiple_of(where_ref[1] * cols, cols), cols)]
    peers = groups - 1
    pack(
        outs[:peers], outs[peers:], [h[...] for h in hids[1:]], [c[...] for c in cots[1:]],
        weight_ref[...], factor, pl.program_id(0), steps,
    )


def near_call(tokens, hids, cots, weight_half, where, factor, tile, frag_cols):
    rows, keys = weight_half.shape
    toks = tokens.shape[0]
    groups = len(cots)
    peers = groups - 1
    steps = rows // tile
    block = pl.BlockSpec((tile, keys), lambda i, w: (i, 0))
    whole = pl.BlockSpec((toks, keys), lambda i, w: (0, 0))
    column = pl.BlockSpec((toks, tile), lambda i, w: (0, i))
    out = pl.pallas_call(
        functools.partial(near_kernel, groups, factor, steps),
        grid_spec=pltpu.PrefetchScalarGridSpec(
            num_scalar_prefetch=1,
            grid=(steps,),
            in_specs=[pl.BlockSpec((toks, tile), lambda i, w: (0, w[0] * steps + i))]
            + [column] * peers
            + [whole] * groups
            + [block],
            out_specs=[block, pl.BlockSpec((tile, frag_cols), lambda i, w: (i, 0))]
            + [pl.BlockSpec((toks, rows + keys), lambda i, w: (0, 0))] * peers,
            scratch_shapes=[pltpu.VMEM((toks, keys), jnp.float32)] * peers,
        ),
        out_shape=[
            jax.ShapeDtypeStruct((rows, keys), jnp.float32),
            jax.ShapeDtypeStruct((rows, frag_cols), jnp.float32),
        ]
        + [jax.ShapeDtypeStruct((toks, rows + keys), jnp.bfloat16)] * peers,
        compiler_params=pltpu.CompilerParams(vmem_limit_bytes=VMEM),
        cost_estimate=SMALL,
    )(where, tokens, *hids, *cots, weight_half)
    return out[0], out[1], list(out[2:])


def last_kernel(factor, steps, low_ref, high_ref, cot_ref, weight_ref, out_ref, acc_ref):
    step = pl.program_id(0)
    hid = jnp.where(step < steps // 2, low_ref[...], high_ref[...])
    pack([out_ref], [acc_ref], [hid], [cot_ref[...]], weight_ref[...], factor, step, steps)


def last_call(hid_low, hid_high, cot, weight_half, factor, tile):
    rows, keys = weight_half.shape
    toks = cot.shape[0]
    steps = rows // tile
    return pl.pallas_call(
        functools.partial(last_kernel, factor, steps),
        grid=(steps,),
        in_specs=[
            pl.BlockSpec((toks, tile), lambda i: (0, jnp.minimum(i, steps // 2 - 1))),
            pl.BlockSpec((toks, tile), lambda i: (0, jnp.maximum(i - steps // 2, 0))),
            pl.BlockSpec((toks, keys), lambda i: (0, 0)),
            pl.BlockSpec((tile, keys), lambda i: (i, 0)),
        ],
        out_specs=pl.BlockSpec((toks, rows + keys), lambda i: (0, 0)),
        out_shape=jax.ShapeDtypeStruct((toks, rows + keys), jnp.bfloat16),
        scratch_shapes=[pltpu.VMEM((toks, keys), jnp.float32)],
        compiler_params=pltpu.CompilerParams(vmem_limit_bytes=32 * MIB),
        cost_estimate=SMALL,
    )(hid_low, hid_high, cot, weight_half)


def adam_step(grad, weight, first, second, scal_ref):
    first = scal_ref[0] * first + scal_ref[1] * grad
    second = scal_ref[2] * second + scal_ref[3] * (grad * grad)
    return 0.99 * weight - 0.1 * (first / (jnp.sqrt(second) + 1e-08))


def frag_kernel(factor, where_ref, scal_ref, low_ref, high_ref, cot_ref, grad_ref, weight_ref, first_ref, second_ref, keep_ref, give_ref):
    chips, size = keep_ref.shape[:2]
    even_mine = where_ref[2] == 0
    half = chips // 2

    for hid_ref, start in ((low_ref, 0), (high_ref, half)):

        @pl.loop(start, start + half)
        def _(j):
            at = pl.ds(pl.multiple_of(2 * j * size, 2 * size), 2 * size)
            hid = hid_ref[:, pl.ds(pl.multiple_of(2 * (j - start) * size, 2 * size), 2 * size)]
            grad = grad_ref[at, :] + row_dot(hid, cot_ref[...], factor)
            inner = adam_step(
                grad, weight_ref[at, :], first_ref[at, :], second_ref[at, :], scal_ref
            )
            even, odd = inner[:size], inner[size:]
            keep_ref[j] = jnp.where(even_mine, even, odd).astype(keep_ref.dtype)
            give_ref[j] = jnp.where(even_mine, odd, even).astype(give_ref.dtype)


def local_call(kernel, outs, *args, smem=1, limit=24):
    vmem = pl.BlockSpec(memory_space=pltpu.VMEM)
    return pl.pallas_call(
        kernel,
        in_specs=[pl.BlockSpec(memory_space=pltpu.SMEM)] * smem + [vmem] * (len(args) - smem),
        out_specs=[vmem] * len(outs),
        out_shape=outs,
        compiler_params=pltpu.CompilerParams(vmem_limit_bytes=limit * MIB),
        cost_estimate=SMALL,
    )(*args)


def frag_call(hid_low, hid_high, cot, grad, weight, first, second, where, scal, factor, own_rows):
    rows, cols = weight.shape
    out = jax.ShapeDtypeStruct((rows // (2 * own_rows), own_rows, cols), jnp.bfloat16)
    return local_call(
        functools.partial(frag_kernel, factor), [out, out],
        where, scal, hid_low, hid_high, cot, grad, weight, first, second, smem=2,
    )


def split_kernel(bit, where_ref, mine_ref, got_ref, stay_ref, leave_ref):
    low = ((where_ref[3] >> bit) & 1) == 0
    for i in range(stay_ref.shape[0]):
        sums = [
            mine_ref[j].astype(jnp.float32) + got_ref[j].astype(jnp.float32)
            for j in (2 * i, 2 * i + 1)
        ]
        stay_ref[i] = jnp.where(low, sums[0], sums[1])
        leave_ref[i] = jnp.where(low, sums[1], sums[0]).astype(leave_ref.dtype)


def split_call(bit, where, mine, got):
    shape = (mine.shape[0] // 2,) + mine.shape[1:]
    return local_call(
        functools.partial(split_kernel, bit),
        [jax.ShapeDtypeStruct(shape, jnp.float32), jax.ShapeDtypeStruct(shape, jnp.bfloat16)],
        where, mine, got,
    )


def halves_kernel(x_ref, y_ref, low_ref, high_ref):
    size = low_ref.shape[0]
    low_ref[...] = y_ref[:size]
    high_ref[...] = x_ref[size:]


def copy_kernel(count, *refs):
    for i in range(count):
        refs[count + i][...] = refs[i][...]


def copy_call(*arrays):
    count = len(arrays)
    rows, cols = arrays[0].shape
    block = pl.BlockSpec((rows // 2, cols), lambda i: (i, 0))
    return pl.pallas_call(
        functools.partial(copy_kernel, count),
        grid=(2,),
        in_specs=[block] * count,
        out_specs=[block] * count,
        out_shape=[jax.ShapeDtypeStruct(x.shape, x.dtype) for x in arrays],
        compiler_params=pltpu.CompilerParams(vmem_limit_bytes=VMEM),
        cost_estimate=SMALL,
    )(*arrays)


def outer_kernel(replicas, where_ref, stay_ref, got_ref, now_ref, mom_ref, _, __, next_ref, next_mom_ref, spread_ref):
    total = stay_ref[0] + got_ref[0].astype(jnp.float32)
    pseudo = now_ref[...] - total / replicas
    moment = 0.9 * mom_ref[...] + pseudo
    outer = now_ref[...] - 0.7 * (pseudo + 0.9 * moment)
    next_ref[...] = outer
    next_mom_ref[...] = moment
    spread_ref[0] = outer.astype(spread_ref.dtype)


def outer_call(replicas, where, stay, got, now, mom, now_copy, mom_copy):
    rows, cols = stay.shape[1:]
    whole = pl.BlockSpec((1, rows, cols), lambda i, w: (0, 0, 0))
    block = pl.BlockSpec((rows, cols), lambda i, w: (0, w[1]))
    anywhere = pl.BlockSpec(memory_space=pl.ANY)
    return pl.pallas_call(
        functools.partial(outer_kernel, replicas),
        grid_spec=pltpu.PrefetchScalarGridSpec(
            num_scalar_prefetch=1,
            grid=(1,),
            in_specs=[whole, whole, block, block, anywhere, anywhere],
            out_specs=[block, block, whole],
        ),
        out_shape=[jax.ShapeDtypeStruct(now.shape, now.dtype)] * 2
        + [jax.ShapeDtypeStruct((1, rows, cols), jnp.bfloat16)],
        input_output_aliases={5: 0, 6: 1},
        cost_estimate=SMALL,
    )(where, stay, got, now, mom, now_copy, mom_copy)


def place_kernel(offsets, final, factor, where_ref, *refs):
    count = len(offsets)
    msgs = refs[:count]
    acc_ref, _, back_ref, keys_ref, sems = refs[count:]
    toks, keys = acc_ref.shape
    rows = msgs[0].shape[1] - keys
    copies = []
    for i, m in enumerate(offsets):
        start = pl.multiple_of((where_ref[0] ^ m) * rows, rows)
        copy = pltpu.make_async_copy(
            msgs[i].at[:, pl.ds(0, rows)], back_ref.at[:, pl.ds(start, rows)], sems.at[i]
        )
        copy.start()
        copies.append(copy)
    total = acc_ref[...]
    for msg in msgs:
        total = total + msg[:, rows:].astype(jnp.float32)
    if final:
        total = total * factor
    keys_ref[...] = total.astype(keys_ref.dtype)
    for copy in copies:
        copy.wait()


def place_call(where, msgs, acc, back, offsets, final, factor):
    vmem = pl.BlockSpec(memory_space=pltpu.VMEM)
    anywhere = pl.BlockSpec(memory_space=pl.ANY)
    count = len(msgs)
    return pl.pallas_call(
        functools.partial(place_kernel, tuple(offsets), final, factor),
        in_specs=[pl.BlockSpec(memory_space=pltpu.SMEM)] + [vmem] * (count + 1) + [anywhere],
        out_specs=[anywhere, vmem],
        out_shape=[
            jax.ShapeDtypeStruct(back.shape, back.dtype),
            jax.ShapeDtypeStruct(acc.shape, jnp.bfloat16 if final else jnp.float32),
        ],
        input_output_aliases={count + 2: 0},
        scratch_shapes=[pltpu.SemaphoreType.DMA((count,))],
        compiler_params=pltpu.CompilerParams(vmem_limit_bytes=24 * MIB),
        cost_estimate=SMALL,
    )(where, *msgs, acc, back)


def adam_kernel(factor, scal_ref, hid_ref, cot_ref, grad_ref, weight_ref, first_ref, second_ref, *rest):
    grad = grad_ref[...] + row_dot(hid_ref[...], cot_ref[...], factor)
    rest[-1][...] = adam_step(grad, weight_ref[...], first_ref[...], second_ref[...], scal_ref)


def adam_call(hid, cot, grad, weight, first, second, scal, factor, tile, lo, hi, skip, base=None):
    rows, keys = weight.shape
    toks = hid.shape[0]
    state = pl.BlockSpec((tile, keys), lambda i: (lo + i, 0))
    in_specs = [
        pl.BlockSpec(memory_space=pltpu.SMEM),
        pl.BlockSpec((toks, tile), lambda i: (0, lo - skip + i)),
        pl.BlockSpec((toks, keys), lambda i: (0, 0)),
    ] + [state] * 4
    args = [scal, hid, cot, grad, weight, first, second]
    aliases = {}
    if base is not None:
        in_specs.append(pl.BlockSpec(memory_space=pl.ANY))
        aliases = {len(args): 0}
        args.append(base)
    return pl.pallas_call(
        functools.partial(adam_kernel, factor),
        grid=(hi - lo,),
        in_specs=in_specs,
        out_specs=state,
        out_shape=jax.ShapeDtypeStruct((rows, keys), jnp.float32),
        input_output_aliases=aliases,
        compiler_params=pltpu.CompilerParams(vmem_limit_bytes=VMEM),
        cost_estimate=SMALL,
    )(*args)


def spread_kernel(bits, where_ref, same_ref, other_ref, base_ref, out_ref, wide_ref, sems):
    chips, size, cols = same_ref.shape
    column = pl.ds(pl.multiple_of(where_ref[1] * cols, cols), cols)
    core = where_ref[2]
    copies = []
    for j in range(chips):
        offset = j ^ where_ref[3]
        at = 0
        for i, k in enumerate(reversed(bits)):
            at = at + (((offset >> k) & 1) << i)
        wide_ref[2 * j + core] = same_ref[at].astype(wide_ref.dtype)
        wide_ref[2 * j + 1 - core] = other_ref[at].astype(wide_ref.dtype)
        for b in (2 * j, 2 * j + 1):
            copy = pltpu.make_async_copy(
                wide_ref.at[b], out_ref.at[pl.ds(b * size, size), column], sems.at[b]
            )
            copy.start()
            copies.append(copy)
    for copy in copies:
        copy.wait()


def spread_call(bits, where, same, other, base):
    chips, size, cols = same.shape
    vmem = pl.BlockSpec(memory_space=pltpu.VMEM)
    anywhere = pl.BlockSpec(memory_space=pl.ANY)
    return pl.pallas_call(
        functools.partial(spread_kernel, bits),
        in_specs=[pl.BlockSpec(memory_space=pltpu.SMEM), vmem, vmem, anywhere],
        out_specs=anywhere,
        out_shape=jax.ShapeDtypeStruct(base.shape, base.dtype),
        input_output_aliases={3: 0},
        scratch_shapes=[
            pltpu.VMEM((2 * chips, size, cols), base.dtype),
            pltpu.SemaphoreType.DMA((2 * chips,)),
        ],
        compiler_params=pltpu.CompilerParams(vmem_limit_bytes=24 * MIB),
        cost_estimate=SMALL,
    )(where, same, other, base)


def per_device(
    hidden,
    key_cotangent,
    local_weight,
    adam_first,
    adam_second,
    outer_weight,
    outer_momentum,
    roster,
    step_count,
):
    tokens = hidden[0]
    cotangent = key_cotangent[0]
    weight = local_weight[0]
    outer_now = outer_weight[0]
    moment_now = outer_momentum[0]
    toks, width = tokens.shape
    rows, keys = weight.shape
    factor = 1.0 / math.sqrt(width)
    frag_cols = keys // FRAGS
    shards = lax.axis_size("fsdp")
    replicas = lax.axis_size("rep")
    shard = lax.axis_index("fsdp")
    replica = lax.axis_index("rep")
    offsets = list(range(1, shards))

    fragment = roster[step_count[0] // FRAGS % ROUNDS, step_count[0] % FRAGS]
    column = fragment * frag_cols
    steps_done = (step_count[0] + 1).astype(jnp.float32)
    scale1 = 1.0 / (1.0 - jnp.power(jnp.float32(0.9), steps_done))
    scale2 = 1.0 / (1.0 - jnp.power(jnp.float32(0.95), steps_done))
    scal = jnp.stack([0.9 * scale1, 0.1 * scale1, 0.95 * scale2, 0.05 * scale2])
    chips = replicas // 2
    core, chip = replica % 2, replica // 2
    own_rows = rows // replicas
    where = jnp.stack([shard, fragment, core, chip]).astype(jnp.int32)
    square = shards == 4
    half = toks // 2
    tile = min(512, rows // 4)
    tile_adam = min(256, rows // 4)
    tiles_adam = rows // tile_adam

    def hid_for(source, m):
        return lax.dynamic_slice_in_dim(source, (shard ^ m) * rows, rows, 1)

    def frag_of(x):
        return lax.dynamic_slice_in_dim(x, column, frag_cols, 1)

    cots = [cotangent] + [pair(cotangent, "fsdp", m) for m in ((1, 2) if square else offsets)]
    hids = [pair(hid_for(tokens, m), "fsdp", m) for m in offsets[:-1]]

    first, second = adam_first[0], adam_second[0]
    weight_half, back_out, key_acc, weight_frag = own_call(
        tokens, cotangent, weight, where, factor, tile, frag_cols
    )
    frag_state = [weight_frag] + list(cut_call(after(where, weight_half), [first, second], frag_cols))
    outer_copy, moment_copy = copy_call(after(outer_now, frag_state[-1]), moment_now)
    last = hid_for(after(tokens, weight_half), offsets[-1])
    lasts = [last[:, : rows // 2], last[:, rows // 2 :]]
    hid_low, hid_high = [pair(x, "fsdp", offsets[-1]) for x in lasts]
    if square:
        out = jax.ShapeDtypeStruct((half, keys), cotangent.dtype)
        low, high = local_call(
            halves_kernel, [out, out], after(cots[1], outer_copy, *lasts), cots[2], smem=0
        )
        cot_lo, cot_hi = pair(low, "fsdp", 1), pair(high, "fsdp", 2)
    near = cots if square else cots[:-1]
    grad, grad_frag, gives = near_call(
        tokens, hids, near, weight_half, after(where, outer_copy), factor, tile, frag_cols
    )
    if square:
        cot_lo, cot_hi = after(cot_lo, grad), after(cot_hi, grad)
        cots.append(jnp.concatenate([cot_lo, cot_hi], axis=0))
    cot_last = cots[-1]
    backs = [pair(x, "fsdp", m) for x, m in zip(gives, offsets)]

    inner, step_at = None, 0

    def inner_step(count, *tokens_ready):
        nonlocal inner, step_at
        end = min(step_at + count, tiles_adam)
        if step_at < end:
            low = end <= tiles_adam // 2
            inner = adam_call(
                after(hid_low if low else hid_high, *tokens_ready), cot_last, grad, weight, first,
                second, scal, factor, tile_adam, step_at, end, 0 if low else tiles_adam // 2,
                base=inner,
            )
            step_at = end
        return inner

    share = tiles_adam // 4
    inner_step(share, *gives)
    hid_high = after(hid_high, inner)

    keep, give = frag_call(
        hid_low, hid_high, frag_of(cot_last), grad_frag, *frag_state, where, scal, factor, own_rows
    )
    got = pair(give, "rep", 1)
    bits = [k for k in range(chips.bit_length()) if (1 << k) < chips]
    for k in bits:
        keep, leave = split_call(k, where, keep, got)
        got = pair(leave, "rep", 2 << k)
        if k == 0:
            got = after(got, inner_step(share, leave))
        elif k == 1:
            give_last = last_call(after(hid_low, leave), hid_high, cot_last, weight_half, factor, tile)
            got = after(got, give_last)
    if len(bits) < 2:
        give_last = last_call(after(hid_low, got), hid_high, cot_last, weight_half, factor, tile)
    backs.append(pair(give_last, "fsdp", offsets[-1]))
    outer_next, moment_next, spread = outer_call(
        replicas, where, keep, got, outer_now, moment_now, outer_copy, moment_copy
    )
    for k in reversed(bits):
        got = pair(spread, "rep", 2 << k)
        got = after(got, inner_step(share if k > 0 else tiles_adam, spread))
        spread = jnp.concatenate([spread, got], axis=0)
        if k == bits[-1]:
            back_out, key_acc = place_call(
                where, [after(b, inner) for b in backs[:-1]], key_acc, back_out, offsets[:-1], False,
                factor,
            )
            spread = after(spread, key_acc)
    got = pair(spread, "rep", 1)
    new_local = spread_call(bits, where, spread, got, inner)
    back_out, keys_out = place_call(
        where, [after(backs[-1], new_local)], key_acc, back_out, offsets[-1:], True, factor
    )

    return (keys_out[None], back_out[None], new_local[None], outer_next[None], moment_next[None])


def solution(mesh):
    in_specs = (
        P("rep", "fsdp", None),
        P("rep", "fsdp", None),
        P("rep", "fsdp", None),
        P("rep", "fsdp", None),
        P("rep", "fsdp", None),
        P("fsdp", "rep", None),
        P("fsdp", "rep", None),
        P(),
        P(),
    )
    out_specs = (
        P("rep", "fsdp", None),
        P("rep", "fsdp", None),
        P("rep", "fsdp", None),
        P("fsdp", "rep", None),
        P("fsdp", "rep", None),
    )
    return jax.shard_map(
        per_device, mesh=mesh, in_specs=in_specs, out_specs=out_specs, check_vma=False
    )
```

```python
import functools
import math

import jax
import jax.numpy as jnp
from jax import lax
from jax.experimental import pallas as pl
from jax.experimental.pallas import tpu as pltpu
from jax.sharding import PartitionSpec as P

FRAGS = 4
ROUNDS = 8
MIB = 1024 * 1024
VMEM = 48 * MIB
SMALL = pl.CostEstimate(flops=1, bytes_accessed=1, transcendentals=0)


def pair(x, axis, offset):
    size = lax.axis_size(axis)
    return lax.ppermute(x, axis, [(i, i ^ offset) for i in range(size)])


def after(x, *others):
    return lax.optimization_barrier((x, *others))[0]


def row_dot(hid, cot, factor):
    part = lax.dot_general(
        hid, cot, (((0,), (0,)), ((), ())), preferred_element_type=jnp.float32
    )
    return (part * factor).astype(jnp.bfloat16).astype(jnp.float32)


def frag_of_ref(ref, where_ref, like_ref):
    cols = like_ref.shape[-1]
    return ref[:, pl.ds(pl.multiple_of(where_ref[1] * cols, cols), cols)]


def part_sum(hids, cots, factor):
    total = row_dot(hids[0][...], cots[0], factor)
    for hid, cot in zip(hids[1:], cots[1:]):
        total = total + row_dot(hid[...], cot, factor)
    return total


def dot_keys(hid, weight):
    return jnp.dot(hid, weight, preferred_element_type=jnp.float32)


def dot_back(cot, weight, factor):
    out = lax.dot_general(
        cot, weight, (((1,), (1,)), ((), ())), preferred_element_type=jnp.float32
    )
    return (out * factor).astype(jnp.bfloat16)


def add_keys(ref, value):
    @pl.when(pl.program_id(0) == 0)
    def _():
        ref[...] = value

    @pl.when(pl.program_id(0) > 0)
    def _():
        ref[...] += value


def send_kernel(peers, where_ref, *refs):
    hids, cot_ref, outs = refs[:peers], refs[peers], refs[peers + 1 :]
    head = pl.program_id(0) == 0
    for hid_ref, out_ref in zip(hids, outs):
        out_ref[...] = jnp.where(head, cot_ref[...], hid_ref[...])


def send_call(tokens, cot, rows, shard, offsets):
    toks, keys = cot.shape
    steps = rows // keys

    def column(m):
        return pl.BlockSpec(
            (toks, keys), lambda i, w, m=m: (0, (w[0] ^ m) * steps + jnp.maximum(i - 1, 0))
        )

    return pl.pallas_call(
        functools.partial(send_kernel, len(offsets)),
        grid_spec=pltpu.PrefetchScalarGridSpec(
            num_scalar_prefetch=1,
            grid=(1 + steps,),
            in_specs=[column(m) for m in offsets] + [pl.BlockSpec((toks, keys), lambda i, w: (0, 0))],
            out_specs=[pl.BlockSpec((toks, keys), lambda i, w: (0, i))] * len(offsets),
        ),
        out_shape=[jax.ShapeDtypeStruct((toks, keys + rows), cot.dtype)] * len(offsets),
        cost_estimate=SMALL,
    )(shard.reshape(1).astype(jnp.int32), *[tokens] * len(offsets), cot)


def own_kernel(factor, where_ref, tokens_ref, cot_ref, weight_ref, half_ref, back_ref, keys_ref):
    half = weight_ref[...].astype(jnp.bfloat16)
    half_ref[...] = half
    back_ref[...] = dot_back(cot_ref[...], half, factor)
    add_keys(keys_ref, dot_keys(tokens_ref[...], half))


def own_call(tokens, cot, weight, where, factor, tile):
    rows, keys = weight.shape
    toks, width = tokens.shape
    steps = rows // tile
    here = pl.BlockSpec((toks, tile), lambda i, w: (0, w[0] * steps + i))
    block = pl.BlockSpec((tile, keys), lambda i, w: (i, 0))
    whole = pl.BlockSpec((toks, keys), lambda i, w: (0, 0))
    return pl.pallas_call(
        functools.partial(own_kernel, factor),
        grid_spec=pltpu.PrefetchScalarGridSpec(
            num_scalar_prefetch=1,
            grid=(steps,),
            in_specs=[here, whole, block],
            out_specs=[block, here, whole],
        ),
        out_shape=[
            jax.ShapeDtypeStruct((rows, keys), jnp.bfloat16),
            jax.ShapeDtypeStruct((toks, width), jnp.bfloat16),
            jax.ShapeDtypeStruct((toks, keys), jnp.float32),
        ],
        compiler_params=pltpu.CompilerParams(vmem_limit_bytes=VMEM),
        cost_estimate=SMALL,
    )(where, tokens, cot, weight)


def pack(outs, accs, hids, cots, weight, factor, step, steps):
    toks = hids[0].shape[0]
    tile = weight.shape[0]
    rows = tile * steps
    at = pl.ds(pl.multiple_of(step * tile, tile), tile)
    back = dot_back(jnp.concatenate(cots, axis=0), weight, factor)
    part = dot_keys(jnp.concatenate(hids, axis=0), weight)
    for g, (out, acc) in enumerate(zip(outs, accs)):
        mine = slice(g * toks, (g + 1) * toks)
        out[:, at] = back[mine]
        add_keys(acc, part[mine])

    @pl.when(step == steps - 1)
    def _():
        for out, acc in zip(outs, accs):
            out[:, rows:] = acc[...].astype(out.dtype)


def near_kernel(groups, factor, steps, where_ref, *refs):
    hids, cots, weight_ref = refs[:groups], refs[groups : 2 * groups], refs[2 * groups]
    frag_ref, *outs = refs[2 * groups + 1 :]
    frag_ref[...] = part_sum(hids, [frag_of_ref(c, where_ref, frag_ref) for c in cots], factor)
    peers = groups - 1
    pack(
        outs[:peers], outs[peers:], [h[...] for h in hids[1:]], [c[...] for c in cots[1:]],
        weight_ref[...], factor, pl.program_id(0), steps,
    )


def near_call(tokens, cot, packs, weight_half, where, factor, tile, frag_cols):
    rows, keys = weight_half.shape
    toks = tokens.shape[0]
    peers = len(packs)
    groups = peers + 1
    steps = rows // tile
    skip = keys // tile
    block = pl.BlockSpec((tile, keys), lambda i, w: (i, 0))
    whole = pl.BlockSpec((toks, keys), lambda i, w: (0, 0))
    column = pl.BlockSpec((toks, tile), lambda i, w: (0, skip + i))
    out = pl.pallas_call(
        functools.partial(near_kernel, groups, factor, steps),
        grid_spec=pltpu.PrefetchScalarGridSpec(
            num_scalar_prefetch=1,
            grid=(steps,),
            in_specs=[pl.BlockSpec((toks, tile), lambda i, w: (0, w[0] * steps + i))]
            + [column] * peers
            + [whole] * groups
            + [block],
            out_specs=[pl.BlockSpec((tile, frag_cols), lambda i, w: (i, 0))]
            + [pl.BlockSpec((toks, rows + keys), lambda i, w: (0, 0))] * peers,
            scratch_shapes=[pltpu.VMEM((toks, keys), jnp.float32)] * peers,
        ),
        out_shape=[jax.ShapeDtypeStruct((rows, frag_cols), jnp.float32)]
        + [jax.ShapeDtypeStruct((toks, rows + keys), jnp.bfloat16)] * peers,
        compiler_params=pltpu.CompilerParams(vmem_limit_bytes=VMEM),
        cost_estimate=SMALL,
    )(where, tokens, *packs, cot, *packs, weight_half)
    return out[0], list(out[1:])


def last_kernel(factor, steps, hid_ref, weight_ref, *refs):
    *cots, out_ref, acc_ref = refs
    cot = jnp.concatenate([c[...] for c in cots], axis=0)
    pack(
        [out_ref], [acc_ref], [hid_ref[...]], [cot], weight_ref[...], factor, pl.program_id(0), steps
    )


def last_call(hid, cots, weight_half, factor, tile):
    rows, keys = weight_half.shape
    toks = hid.shape[0]
    steps = rows // tile
    return pl.pallas_call(
        functools.partial(last_kernel, factor, steps),
        grid=(steps,),
        in_specs=[
            pl.BlockSpec((toks, tile), lambda i: (0, i)),
            pl.BlockSpec((tile, keys), lambda i: (i, 0)),
        ]
        + [pl.BlockSpec(c.shape, lambda i: (0, 0)) for c in cots],
        out_specs=pl.BlockSpec((toks, rows + keys), lambda i: (0, 0)),
        out_shape=jax.ShapeDtypeStruct((toks, rows + keys), jnp.bfloat16),
        scratch_shapes=[pltpu.VMEM((toks, keys), jnp.float32)],
        compiler_params=pltpu.CompilerParams(vmem_limit_bytes=32 * MIB),
        cost_estimate=SMALL,
    )(hid, weight_half, *cots)


def adam_step(grad, weight, first, second, scal_ref):
    first = scal_ref[0] * first + scal_ref[1] * grad
    second = scal_ref[2] * second + scal_ref[3] * (grad * grad)
    return 0.99 * weight - 0.1 * (first / (jnp.sqrt(second) + 1e-08))


def frag_kernel(factor, where_ref, scal_ref, hid_ref, *refs):
    *cots, grad_ref, weight_ref, first_ref, second_ref, keep_ref, give_ref, here_ref, sems = refs
    chips, size = keep_ref.shape[:2]
    cols = keep_ref.shape[2]
    even_mine = where_ref[2] == 0
    column = pl.ds(pl.multiple_of(where_ref[1] * cols, cols), cols)
    copies = []
    for j in range(chips):
        at = pl.ds(2 * j * size, 2 * size)
        sources = [grad_ref.at[at, :]] + [
            x.at[at, column] for x in (weight_ref, first_ref, second_ref)
        ]
        copies.append(
            [
                pltpu.make_async_copy(source, here_ref.at[i, at, :], sems.at[i, j])
                for i, source in enumerate(sources)
            ]
        )
        for copy in copies[-1]:
            copy.start()
    cot = jnp.concatenate([c[:, column] for c in cots], axis=0)
    for j in range(chips):
        at = pl.ds(2 * j * size, 2 * size)
        part = row_dot(hid_ref[:, at], cot, factor)
        for copy in copies[j]:
            copy.wait()
        inner = adam_step(
            here_ref[0, at, :] + part, here_ref[1, at, :], here_ref[2, at, :], here_ref[3, at, :],
            scal_ref,
        )
        even, odd = inner[:size], inner[size:]
        keep_ref[j] = jnp.where(even_mine, even, odd).astype(keep_ref.dtype)
        give_ref[j] = jnp.where(even_mine, odd, even).astype(give_ref.dtype)


def local_call(kernel, outs, *args, smem=1, limit=24):
    vmem = pl.BlockSpec(memory_space=pltpu.VMEM)
    return pl.pallas_call(
        kernel,
        in_specs=[pl.BlockSpec(memory_space=pltpu.SMEM)] * smem + [vmem] * (len(args) - smem),
        out_specs=[vmem] * len(outs),
        out_shape=outs,
        compiler_params=pltpu.CompilerParams(vmem_limit_bytes=limit * MIB),
        cost_estimate=SMALL,
    )(*args)


def frag_call(hid, cots, grad, weight, first, second, where, scal, factor, own_rows):
    rows, cols = grad.shape
    chips = rows // (2 * own_rows)
    vmem = pl.BlockSpec(memory_space=pltpu.VMEM)
    out = jax.ShapeDtypeStruct((chips, own_rows, cols), jnp.bfloat16)
    return pl.pallas_call(
        functools.partial(frag_kernel, factor),
        in_specs=[pl.BlockSpec(memory_space=pltpu.SMEM)] * 2
        + [vmem] * (1 + len(cots))
        + [pl.BlockSpec(memory_space=pl.ANY)] * 4,
        out_specs=[vmem, vmem],
        out_shape=[out, out],
        scratch_shapes=[
            pltpu.VMEM((4, rows, cols), jnp.float32), pltpu.SemaphoreType.DMA((4, chips))
        ],
        compiler_params=pltpu.CompilerParams(vmem_limit_bytes=VMEM),
        cost_estimate=SMALL,
    )(where, scal, hid, *cots, grad, weight, first, second)


def split_kernel(bit, where_ref, mine_ref, got_ref, stay_ref, leave_ref):
    low = ((where_ref[3] >> bit) & 1) == 0
    for i in range(stay_ref.shape[0]):
        sums = [
            mine_ref[j].astype(jnp.float32) + got_ref[j].astype(jnp.float32)
            for j in (2 * i, 2 * i + 1)
        ]
        stay_ref[i] = jnp.where(low, sums[0], sums[1])
        leave_ref[i] = jnp.where(low, sums[1], sums[0]).astype(leave_ref.dtype)


def split_call(bit, where, mine, got):
    shape = (mine.shape[0] // 2,) + mine.shape[1:]
    return local_call(
        functools.partial(split_kernel, bit),
        [jax.ShapeDtypeStruct(shape, jnp.float32), jax.ShapeDtypeStruct(shape, jnp.bfloat16)],
        where, mine, got,
    )


def halves_kernel(x_ref, y_ref, low_ref, high_ref):
    low_ref[...] = y_ref[...]
    high_ref[...] = x_ref[...]


def halves_call(pack_x, pack_y, keys):
    half = pack_x.shape[0] // 2
    first = pl.BlockSpec((half, keys), lambda i: (0, 0))
    second = pl.BlockSpec((half, keys), lambda i: (1, 0))
    return pl.pallas_call(
        halves_kernel,
        grid=(1,),
        in_specs=[second, first],
        out_specs=[first, first],
        out_shape=[jax.ShapeDtypeStruct((half, keys), pack_x.dtype)] * 2,
        cost_estimate=SMALL,
    )(pack_x, pack_y)


def copy_kernel(count, where_ref, *refs):
    for i in range(count):
        refs[count + i][...] = refs[i][...]
        refs[2 * count + i][...] = frag_of_ref(refs[i], where_ref, refs[2 * count + i])


def copy_call(where, arrays, frag_cols):
    count = len(arrays)
    rows, cols = arrays[0].shape
    block = pl.BlockSpec((rows // 2, cols), lambda i, w: (i, 0))
    part = pl.BlockSpec((rows // 2, frag_cols), lambda i, w: (i, 0))
    return pl.pallas_call(
        functools.partial(copy_kernel, count),
        grid_spec=pltpu.PrefetchScalarGridSpec(
            num_scalar_prefetch=1,
            grid=(2,),
            in_specs=[block] * count,
            out_specs=[block] * count + [part] * count,
        ),
        out_shape=[jax.ShapeDtypeStruct(x.shape, x.dtype) for x in arrays]
        + [jax.ShapeDtypeStruct((rows, frag_cols), x.dtype) for x in arrays],
        compiler_params=pltpu.CompilerParams(vmem_limit_bytes=VMEM),
        cost_estimate=SMALL,
    )(where, *arrays)


def outer_step(replicas, stay_ref, got_ref, now_ref, mom_ref):
    total = stay_ref[0] + got_ref[0].astype(jnp.float32)
    pseudo = now_ref[...] - total / replicas
    moment = 0.9 * mom_ref[...] + pseudo
    return now_ref[...] - 0.7 * (pseudo + 0.9 * moment), moment


def outer_kernel(replicas, *refs):
    spread_ref = refs[-1]
    spread_ref[0] = outer_step(replicas, *refs[:-1])[0].astype(spread_ref.dtype)


def outer_call(replicas, stay, got, now, mom):
    return local_call(
        functools.partial(outer_kernel, replicas),
        [jax.ShapeDtypeStruct(got.shape, got.dtype)],
        stay, got, now, mom, smem=0,
    )[0]


def put_kernel(replicas, where_ref, stay_ref, got_ref, now_ref, mom_ref, _, __, out_ref, out_mom_ref, outer_ref, moment_ref, sems):
    outer_ref[...], moment_ref[...] = outer_step(replicas, stay_ref, got_ref, now_ref, mom_ref)
    cols = now_ref.shape[1]
    at = pl.ds(pl.multiple_of(where_ref[1] * cols, cols), cols)
    copies = [
        pltpu.make_async_copy(outer_ref, out_ref.at[:, at], sems.at[0]),
        pltpu.make_async_copy(moment_ref, out_mom_ref.at[:, at], sems.at[1]),
    ]
    for copy in copies:
        copy.start()
    for copy in copies:
        copy.wait()


def put_call(replicas, where, stay, got, now, mom, now_copy, mom_copy):
    vmem = pl.BlockSpec(memory_space=pltpu.VMEM)
    anywhere = pl.BlockSpec(memory_space=pl.ANY)
    return pl.pallas_call(
        functools.partial(put_kernel, replicas),
        in_specs=[pl.BlockSpec(memory_space=pltpu.SMEM)] + [vmem] * 4 + [anywhere] * 2,
        out_specs=[anywhere] * 2,
        out_shape=[jax.ShapeDtypeStruct(now_copy.shape, now_copy.dtype)] * 2,
        input_output_aliases={5: 0, 6: 1},
        scratch_shapes=[pltpu.VMEM(now.shape, now.dtype)] * 2 + [pltpu.SemaphoreType.DMA((2,))],
        compiler_params=pltpu.CompilerParams(vmem_limit_bytes=24 * MIB),
        cost_estimate=SMALL,
    )(where, stay, got, now, mom, now_copy, mom_copy)


def place_kernel(offsets, final, factor, where_ref, *refs):
    count = len(offsets)
    msgs = refs[:count]
    acc_ref, _, back_ref, keys_ref, sems = refs[count:]
    toks, keys = acc_ref.shape
    rows = msgs[0].shape[1] - keys
    copies = []
    for i, m in enumerate(offsets):
        start = pl.multiple_of((where_ref[0] ^ m) * rows, rows)
        copy = pltpu.make_async_copy(
            msgs[i].at[:, pl.ds(0, rows)], back_ref.at[:, pl.ds(start, rows)], sems.at[i]
        )
        copy.start()
        copies.append(copy)
    total = acc_ref[...]
    for msg in msgs:
        total = total + msg[:, rows:].astype(jnp.float32)
    if final:
        total = total * factor
    keys_ref[...] = total.astype(keys_ref.dtype)
    for copy in copies:
        copy.wait()


def place_call(where, msgs, acc, back, offsets, final, factor):
    vmem = pl.BlockSpec(memory_space=pltpu.VMEM)
    anywhere = pl.BlockSpec(memory_space=pl.ANY)
    count = len(msgs)
    return pl.pallas_call(
        functools.partial(place_kernel, tuple(offsets), final, factor),
        in_specs=[pl.BlockSpec(memory_space=pltpu.SMEM)] + [vmem] * (count + 1) + [anywhere],
        out_specs=[anywhere, vmem],
        out_shape=[
            jax.ShapeDtypeStruct(back.shape, back.dtype),
            jax.ShapeDtypeStruct(acc.shape, jnp.bfloat16 if final else jnp.float32),
        ],
        input_output_aliases={count + 2: 0},
        scratch_shapes=[pltpu.SemaphoreType.DMA((count,))],
        compiler_params=pltpu.CompilerParams(vmem_limit_bytes=24 * MIB),
        cost_estimate=SMALL,
    )(where, *msgs, acc, back)


def adam_kernel(groups, pieces, factor, where_ref, scal_ref, *refs):
    hids, refs = refs[:groups], refs[groups:]
    cots = [c[...] for c in refs[: groups - 1]]
    weight_ref, first_ref, second_ref = refs[groups - 1 : groups + 2]
    *rest, out_ref = refs[groups + 2 :]
    cots.append(jnp.concatenate([c[...] for c in rest[:pieces]], axis=0))
    grad = part_sum(hids, cots, factor)
    out_ref[...] = adam_step(grad, weight_ref[...], first_ref[...], second_ref[...], scal_ref)


def adam_call(tokens, cot, packs, hid_last, cot_last, weight, first, second, where, scal, factor, frag_cols, part, *base):
    rows, keys = weight.shape
    toks = tokens.shape[0]
    tile = min(1024, rows // 2)
    steps = rows // tile
    lo = part * (steps // 2)
    skip = keys // tile
    groups = len(packs) + 2

    def col(j, w):
        return j + (j >= w[1]).astype(jnp.int32)

    def block(height):
        return pl.BlockSpec((height, frag_cols), lambda i, j, w: (0, col(j, w)))

    state = pl.BlockSpec((tile, frag_cols), lambda i, j, w: (lo + i, col(j, w)))
    return pl.pallas_call(
        functools.partial(adam_kernel, groups, len(cot_last), factor),
        grid_spec=pltpu.PrefetchScalarGridSpec(
            num_scalar_prefetch=1,
            grid=(steps // 2, keys // frag_cols - 1),
            in_specs=[
                pl.BlockSpec(memory_space=pltpu.SMEM),
                pl.BlockSpec((toks, tile), lambda i, j, w: (0, w[0] * steps + lo + i)),
            ]
            + [pl.BlockSpec((toks, tile), lambda i, j, w: (0, skip + lo + i))] * len(packs)
            + [pl.BlockSpec((toks, tile), lambda i, j, w: (0, lo + i))]
            + [block(toks)] * (groups - 1)
            + [state] * 3
            + [block(c.shape[0]) for c in cot_last]
            + [pl.BlockSpec(memory_space=pl.ANY)] * len(base),
            out_specs=state,
        ),
        out_shape=jax.ShapeDtypeStruct((rows, keys), jnp.float32),
        input_output_aliases={4 + 2 * groups + len(cot_last): 0} if base else {},
        compiler_params=pltpu.CompilerParams(vmem_limit_bytes=VMEM),
        cost_estimate=SMALL,
    )(where, scal, tokens, *packs, hid_last, cot, *packs, weight, first, second, *cot_last, *base)


def spread_kernel(bits, where_ref, same_ref, other_ref, base_ref, out_ref, wide_ref, sems):
    chips, size, cols = same_ref.shape
    column = pl.ds(pl.multiple_of(where_ref[1] * cols, cols), cols)
    core = where_ref[2]
    copies = []
    for j in range(chips):
        offset = j ^ where_ref[3]
        at = 0
        for i, k in enumerate(reversed(bits)):
            at = at + (((offset >> k) & 1) << i)
        wide_ref[2 * j + core] = same_ref[at].astype(wide_ref.dtype)
        wide_ref[2 * j + 1 - core] = other_ref[at].astype(wide_ref.dtype)
        for b in (2 * j, 2 * j + 1):
            copy = pltpu.make_async_copy(
                wide_ref.at[b], out_ref.at[pl.ds(b * size, size), column], sems.at[b]
            )
            copy.start()
            copies.append(copy)
    for copy in copies:
        copy.wait()


def spread_call(bits, where, same, other, base):
    chips, size, cols = same.shape
    vmem = pl.BlockSpec(memory_space=pltpu.VMEM)
    anywhere = pl.BlockSpec(memory_space=pl.ANY)
    return pl.pallas_call(
        functools.partial(spread_kernel, bits),
        in_specs=[pl.BlockSpec(memory_space=pltpu.SMEM), vmem, vmem, anywhere],
        out_specs=anywhere,
        out_shape=jax.ShapeDtypeStruct(base.shape, base.dtype),
        input_output_aliases={3: 0},
        scratch_shapes=[
            pltpu.VMEM((2 * chips, size, cols), base.dtype),
            pltpu.SemaphoreType.DMA((2 * chips,)),
        ],
        compiler_params=pltpu.CompilerParams(vmem_limit_bytes=24 * MIB),
        cost_estimate=SMALL,
    )(where, same, other, base)


def per_device(
    hidden,
    key_cotangent,
    local_weight,
    adam_first,
    adam_second,
    outer_weight,
    outer_momentum,
    roster,
    step_count,
):
    tokens = hidden[0]
    cotangent = key_cotangent[0]
    weight = local_weight[0]
    outer_now = outer_weight[0]
    moment_now = outer_momentum[0]
    toks, width = tokens.shape
    rows, keys = weight.shape
    factor = 1.0 / math.sqrt(width)
    frag_cols = keys // FRAGS
    shards = lax.axis_size("fsdp")
    replicas = lax.axis_size("rep")
    shard = lax.axis_index("fsdp")
    replica = lax.axis_index("rep")
    offsets = list(range(1, shards))

    fragment = roster[step_count[0] // FRAGS % ROUNDS, step_count[0] % FRAGS]
    steps_done = (step_count[0] + 1).astype(jnp.float32)
    scale1 = 1.0 / (1.0 - jnp.power(jnp.float32(0.9), steps_done))
    scale2 = 1.0 / (1.0 - jnp.power(jnp.float32(0.95), steps_done))
    scal = jnp.stack([0.9 * scale1, 0.1 * scale1, 0.95 * scale2, 0.05 * scale2])
    chips = replicas // 2
    core, chip = replica % 2, replica // 2
    own_rows = rows // replicas
    where = jnp.stack([shard, fragment, core, chip]).astype(jnp.int32)
    square = shards == 4
    tile = min(512, rows // 4)

    def hid_for(source, m):
        return lax.dynamic_slice_in_dim(source, (shard ^ m) * rows, rows, 1)

    sends = send_call(tokens, cotangent, rows, shard, offsets[:-1])
    packs = [pair(x, "fsdp", m) for x, m in zip(sends, offsets)]

    first, second = adam_first[0], adam_second[0]
    weight_half, back_out, key_acc = own_call(tokens, cotangent, weight, where, factor, tile)
    outer_copy, moment_copy, *outer_frag = copy_call(
        after(where, weight_half), [outer_now, moment_now], frag_cols
    )
    hid_last = hid_for(after(tokens, weight_half), offsets[-1])
    hid_last = pair(after(hid_last, outer_copy, *packs), "fsdp", offsets[-1])
    if square:
        low, high = halves_call(after(packs[0], outer_copy), packs[1], keys)
        cot_last = [pair(low, "fsdp", 1), pair(high, "fsdp", 2)]
    else:
        cot_last = [pair(cotangent, "fsdp", offsets[-1])]
    grad_frag, gives = near_call(
        tokens, cotangent, packs, weight_half, after(where, outer_copy), factor, tile, frag_cols
    )
    backs = [pair(x, "fsdp", m) for x, m in zip(gives, offsets)]
    cot_last = [after(c, *gives) for c in cot_last]

    def inner_half(part, hid, *base):
        return adam_call(
            tokens, cotangent, packs, hid, cot_last, weight, first, second, where, scal, factor,
            frag_cols, part, *base,
        )

    keep, give = frag_call(
        hid_last, cot_last, grad_frag, weight, first, second, where, scal, factor, own_rows
    )
    got = pair(give, "rep", 1)
    bits = [k for k in range(chips.bit_length()) if (1 << k) < chips]
    for k in bits:
        keep, leave = split_call(k, where, keep, got)
        got = pair(leave, "rep", 2 << k)
        if k == 0:
            give_last = last_call(after(hid_last, leave), cot_last, weight_half, factor, tile)
            got = after(got, give_last)
        if k == bits[-1]:
            inner = inner_half(0, after(hid_last, leave, give_last))
            got = after(got, inner)
    backs.append(pair(give_last, "fsdp", offsets[-1]))
    outer_args = (keep, got, *outer_frag)
    spread = outer_call(replicas, *outer_args)
    for k in reversed(bits):
        got = pair(spread, "rep", 2 << k)
        if k == bits[-1]:
            outer_next, moment_next = put_call(
                replicas, where, after(keep, spread), *outer_args[1:], outer_copy, moment_copy
            )
            back_out, key_acc = place_call(
                where, [after(b, outer_next) for b in backs[:-1]], key_acc, back_out, offsets[:-1],
                False, factor,
            )
            got = after(got, key_acc)
        if k == 0:
            inner = inner_half(1, after(hid_last, spread), inner)
            got = after(got, inner)
        spread = jnp.concatenate([spread, got], axis=0)
    got = pair(spread, "rep", 1)
    new_local = spread_call(bits, where, spread, got, inner)
    back_out, keys_out = place_call(
        where, [after(backs[-1], new_local)], key_acc, back_out, offsets[-1:], True, factor
    )

    return (keys_out[None], back_out[None], new_local[None], outer_next[None], moment_next[None])


def solution(mesh):
    in_specs = (
        P("rep", "fsdp", None),
        P("rep", "fsdp", None),
        P("rep", "fsdp", None),
        P("rep", "fsdp", None),
        P("rep", "fsdp", None),
        P("fsdp", "rep", None),
        P("fsdp", "rep", None),
        P(),
        P(),
    )
    out_specs = (
        P("rep", "fsdp", None),
        P("rep", "fsdp", None),
        P("rep", "fsdp", None),
        P("fsdp", "rep", None),
        P("fsdp", "rep", None),
    )
    return jax.shard_map(
        per_device, mesh=mesh, in_specs=in_specs, out_specs=out_specs, check_vma=False
    )
```

```python
import functools
import math

import jax
import jax.numpy as jnp
from jax import lax
from jax.experimental import pallas as pl
from jax.experimental.pallas import tpu as pltpu
from jax.sharding import PartitionSpec as P

FRAGS = 4
ROUNDS = 8
MIB = 1024 * 1024
VMEM = 48 * MIB
SMALL = pl.CostEstimate(flops=1, bytes_accessed=1, transcendentals=0)


def pair(x, axis, offset):
    size = lax.axis_size(axis)
    return lax.ppermute(x, axis, [(i, i ^ offset) for i in range(size)])


def after(x, *others):
    return lax.optimization_barrier((x, *others))[0]


def row_dot(hid, cot, factor):
    part = lax.dot_general(
        hid, cot, (((0,), (0,)), ((), ())), preferred_element_type=jnp.float32
    )
    return (part * factor).astype(jnp.bfloat16).astype(jnp.float32)


def frag_of_ref(ref, where_ref, like_ref):
    cols = like_ref.shape[-1]
    return ref[:, pl.ds(pl.multiple_of(where_ref[1] * cols, cols), cols)]


def part_sum(hids, cots, factor):
    total = row_dot(hids[0][...], cots[0], factor)
    for hid, cot in zip(hids[1:], cots[1:]):
        total = total + row_dot(hid[...], cot, factor)
    return total


def dot_keys(hid, weight):
    return jnp.dot(hid, weight, preferred_element_type=jnp.float32)


def dot_back(cot, weight, factor):
    out = lax.dot_general(
        cot, weight, (((1,), (1,)), ((), ())), preferred_element_type=jnp.float32
    )
    return (out * factor).astype(jnp.bfloat16)


def add_keys(ref, value):
    @pl.when(pl.program_id(0) == 0)
    def _():
        ref[...] = value

    @pl.when(pl.program_id(0) > 0)
    def _():
        ref[...] += value


def own_kernel(factor, where_ref, tokens_ref, cot_ref, weight_ref, half_ref, back_ref, keys_ref):
    half = weight_ref[...].astype(jnp.bfloat16)
    half_ref[...] = half
    back_ref[...] = dot_back(cot_ref[...], half, factor)
    add_keys(keys_ref, dot_keys(tokens_ref[...], half))


def own_call(tokens, cot, weight, where, factor, tile):
    rows, keys = weight.shape
    toks, width = tokens.shape
    steps = rows // tile
    here = pl.BlockSpec((toks, tile), lambda i, w: (0, w[0] * steps + i))
    block = pl.BlockSpec((tile, keys), lambda i, w: (i, 0))
    whole = pl.BlockSpec((toks, keys), lambda i, w: (0, 0))
    return pl.pallas_call(
        functools.partial(own_kernel, factor),
        grid_spec=pltpu.PrefetchScalarGridSpec(
            num_scalar_prefetch=1,
            grid=(steps,),
            in_specs=[here, whole, block],
            out_specs=[block, here, whole],
        ),
        out_shape=[
            jax.ShapeDtypeStruct((rows, keys), jnp.bfloat16),
            jax.ShapeDtypeStruct((toks, width), jnp.bfloat16),
            jax.ShapeDtypeStruct((toks, keys), jnp.float32),
        ],
        compiler_params=pltpu.CompilerParams(vmem_limit_bytes=VMEM),
        cost_estimate=SMALL,
    )(where, tokens, cot, weight)


def pack(outs, accs, hids, cots, weight, factor, step, steps):
    toks = hids[0].shape[0]
    tile = weight.shape[0]
    rows = tile * steps
    at = pl.ds(pl.multiple_of(step * tile, tile), tile)
    back = dot_back(jnp.concatenate(cots, axis=0), weight, factor)
    part = dot_keys(jnp.concatenate(hids, axis=0), weight)
    for g, (out, acc) in enumerate(zip(outs, accs)):
        mine = slice(g * toks, (g + 1) * toks)
        out[:, at] = back[mine]
        add_keys(acc, part[mine])

    @pl.when(step == steps - 1)
    def _():
        for out, acc in zip(outs, accs):
            out[:, rows:] = acc[...].astype(out.dtype)


def near_kernel(groups, factor, steps, where_ref, *refs):
    hids, cots, weight_ref = refs[:groups], refs[groups : 2 * groups], refs[2 * groups]
    frag_ref, *outs = refs[2 * groups + 1 :]
    frag_ref[...] = part_sum(hids, [frag_of_ref(c, where_ref, frag_ref) for c in cots], factor)
    peers = groups - 1
    pack(
        outs[:peers], outs[peers:], [h[...] for h in hids[1:]], [c[...] for c in cots[1:]],
        weight_ref[...], factor, pl.program_id(0), steps,
    )


def near_call(tokens, cot, packs, weight_half, where, factor, tile, frag_cols):
    rows, keys = weight_half.shape
    toks = tokens.shape[0]
    peers = len(packs)
    groups = peers + 1
    steps = rows // tile
    skip = keys // tile
    block = pl.BlockSpec((tile, keys), lambda i, w: (i, 0))
    whole = pl.BlockSpec((toks, keys), lambda i, w: (0, 0))
    column = pl.BlockSpec((toks, tile), lambda i, w: (0, skip + i))
    out = pl.pallas_call(
        functools.partial(near_kernel, groups, factor, steps),
        grid_spec=pltpu.PrefetchScalarGridSpec(
            num_scalar_prefetch=1,
            grid=(steps,),
            in_specs=[pl.BlockSpec((toks, tile), lambda i, w: (0, w[0] * steps + i))]
            + [column] * peers
            + [whole] * groups
            + [block],
            out_specs=[pl.BlockSpec((tile, frag_cols), lambda i, w: (i, w[1]))]
            + [pl.BlockSpec((toks, rows + keys), lambda i, w: (0, 0))] * peers,
            scratch_shapes=[pltpu.VMEM((toks, keys), jnp.float32)] * peers,
        ),
        out_shape=[jax.ShapeDtypeStruct((rows, keys), jnp.float32)]
        + [jax.ShapeDtypeStruct((toks, rows + keys), jnp.bfloat16)] * peers,
        compiler_params=pltpu.CompilerParams(vmem_limit_bytes=VMEM),
        cost_estimate=SMALL,
    )(where, tokens, *packs, cot, *packs, weight_half)
    return out[0], list(out[1:])


def last_kernel(factor, steps, hid_ref, weight_ref, *refs):
    *cots, out_ref, acc_ref = refs
    cot = jnp.concatenate([c[...] for c in cots], axis=0)
    pack(
        [out_ref], [acc_ref], [hid_ref[...]], [cot], weight_ref[...], factor, pl.program_id(0), steps
    )


def last_call(hid, cots, weight_half, factor, tile):
    rows, keys = weight_half.shape
    toks = hid.shape[0]
    steps = rows // tile
    return pl.pallas_call(
        functools.partial(last_kernel, factor, steps),
        grid=(steps,),
        in_specs=[
            pl.BlockSpec((toks, tile), lambda i: (0, i)),
            pl.BlockSpec((tile, keys), lambda i: (i, 0)),
        ]
        + [pl.BlockSpec(c.shape, lambda i: (0, 0)) for c in cots],
        out_specs=pl.BlockSpec((toks, rows + keys), lambda i: (0, 0)),
        out_shape=jax.ShapeDtypeStruct((toks, rows + keys), jnp.bfloat16),
        scratch_shapes=[pltpu.VMEM((toks, keys), jnp.float32)],
        compiler_params=pltpu.CompilerParams(vmem_limit_bytes=32 * MIB),
        cost_estimate=SMALL,
    )(hid, weight_half, *cots)


def adam_step(grad, weight, first, second, scal_ref):
    first = scal_ref[0] * first + scal_ref[1] * grad
    second = scal_ref[2] * second + scal_ref[3] * (grad * grad)
    return 0.99 * weight - 0.1 * (first / (jnp.sqrt(second) + 1e-08))


def frag_kernel(factor, where_ref, scal_ref, hid_ref, *refs):
    *cots, grad_ref, weight_ref, first_ref, second_ref, keep_ref, give_ref, here_ref, sems = refs
    chips, size = keep_ref.shape[:2]
    cols = keep_ref.shape[2]
    even_mine = where_ref[2] == 0
    column = pl.ds(pl.multiple_of(where_ref[1] * cols, cols), cols)
    copies = []
    for j in range(chips):
        at = pl.ds(2 * j * size, 2 * size)
        sources = [x.at[at, column] for x in (grad_ref, weight_ref, first_ref, second_ref)]
        copies.append(
            [
                pltpu.make_async_copy(source, here_ref.at[i, at, :], sems.at[i, j])
                for i, source in enumerate(sources)
            ]
        )
        for copy in copies[-1]:
            copy.start()
    cot = jnp.concatenate([c[:, column] for c in cots], axis=0)
    for j in range(chips):
        at = pl.ds(2 * j * size, 2 * size)
        part = row_dot(hid_ref[:, at], cot, factor)
        for copy in copies[j]:
            copy.wait()
        inner = adam_step(
            here_ref[0, at, :] + part, here_ref[1, at, :], here_ref[2, at, :], here_ref[3, at, :],
            scal_ref,
        )
        even, odd = inner[:size], inner[size:]
        keep_ref[j] = jnp.where(even_mine, even, odd).astype(keep_ref.dtype)
        give_ref[j] = jnp.where(even_mine, odd, even).astype(give_ref.dtype)


def local_call(kernel, outs, *args, smem=1, limit=24):
    vmem = pl.BlockSpec(memory_space=pltpu.VMEM)
    return pl.pallas_call(
        kernel,
        in_specs=[pl.BlockSpec(memory_space=pltpu.SMEM)] * smem + [vmem] * (len(args) - smem),
        out_specs=[vmem] * len(outs),
        out_shape=outs,
        compiler_params=pltpu.CompilerParams(vmem_limit_bytes=limit * MIB),
        cost_estimate=SMALL,
    )(*args)


def frag_call(hid, cots, grad, weight, first, second, where, scal, factor, own_rows, cols):
    rows = grad.shape[0]
    chips = rows // (2 * own_rows)
    vmem = pl.BlockSpec(memory_space=pltpu.VMEM)
    out = jax.ShapeDtypeStruct((chips, own_rows, cols), jnp.bfloat16)
    return pl.pallas_call(
        functools.partial(frag_kernel, factor),
        in_specs=[pl.BlockSpec(memory_space=pltpu.SMEM)] * 2
        + [vmem] * (1 + len(cots))
        + [pl.BlockSpec(memory_space=pl.ANY)] * 4,
        out_specs=[vmem, vmem],
        out_shape=[out, out],
        scratch_shapes=[
            pltpu.VMEM((4, rows, cols), jnp.float32), pltpu.SemaphoreType.DMA((4, chips))
        ],
        compiler_params=pltpu.CompilerParams(vmem_limit_bytes=VMEM),
        cost_estimate=SMALL,
    )(where, scal, hid, *cots, grad, weight, first, second)


def split_kernel(bit, where_ref, mine_ref, got_ref, stay_ref, leave_ref):
    low = ((where_ref[3] >> bit) & 1) == 0
    for i in range(stay_ref.shape[0]):
        sums = [
            mine_ref[j].astype(jnp.float32) + got_ref[j].astype(jnp.float32)
            for j in (2 * i, 2 * i + 1)
        ]
        stay_ref[i] = jnp.where(low, sums[0], sums[1])
        leave_ref[i] = jnp.where(low, sums[1], sums[0]).astype(leave_ref.dtype)


def split_call(bit, where, mine, got):
    shape = (mine.shape[0] // 2,) + mine.shape[1:]
    return local_call(
        functools.partial(split_kernel, bit),
        [jax.ShapeDtypeStruct(shape, jnp.float32), jax.ShapeDtypeStruct(shape, jnp.bfloat16)],
        where, mine, got,
    )


def halves_kernel(x_ref, y_ref, low_ref, high_ref):
    low_ref[...] = y_ref[...]
    high_ref[...] = x_ref[...]


def halves_call(pack_x, pack_y, keys):
    half = pack_x.shape[0] // 2
    first = pl.BlockSpec((half, keys), lambda i: (0, 0))
    second = pl.BlockSpec((half, keys), lambda i: (1, 0))
    return pl.pallas_call(
        halves_kernel,
        grid=(1,),
        in_specs=[second, first],
        out_specs=[first, first],
        out_shape=[jax.ShapeDtypeStruct((half, keys), pack_x.dtype)] * 2,
        cost_estimate=SMALL,
    )(pack_x, pack_y)


def copy_kernel(count, where_ref, *refs):
    for i in range(count):
        refs[count + i][...] = refs[i][...]
        refs[2 * count + i][...] = frag_of_ref(refs[i], where_ref, refs[2 * count + i])


def copy_call(where, arrays, frag_cols):
    count = len(arrays)
    rows, cols = arrays[0].shape
    block = pl.BlockSpec((rows // 2, cols), lambda i, w: (i, 0))
    part = pl.BlockSpec((rows // 2, frag_cols), lambda i, w: (i, 0))
    return pl.pallas_call(
        functools.partial(copy_kernel, count),
        grid_spec=pltpu.PrefetchScalarGridSpec(
            num_scalar_prefetch=1,
            grid=(2,),
            in_specs=[block] * count,
            out_specs=[block] * count + [part] * count,
        ),
        out_shape=[jax.ShapeDtypeStruct(x.shape, x.dtype) for x in arrays]
        + [jax.ShapeDtypeStruct((rows, frag_cols), x.dtype) for x in arrays],
        compiler_params=pltpu.CompilerParams(vmem_limit_bytes=VMEM),
        cost_estimate=SMALL,
    )(where, *arrays)


def outer_step(replicas, stay_ref, got_ref, now_ref, mom_ref):
    total = stay_ref[0] + got_ref[0].astype(jnp.float32)
    pseudo = now_ref[...] - total / replicas
    moment = 0.9 * mom_ref[...] + pseudo
    return now_ref[...] - 0.7 * (pseudo + 0.9 * moment), moment


def outer_kernel(replicas, *refs):
    spread_ref = refs[-1]
    spread_ref[0] = outer_step(replicas, *refs[:-1])[0].astype(spread_ref.dtype)


def outer_call(replicas, stay, got, now, mom):
    return local_call(
        functools.partial(outer_kernel, replicas),
        [jax.ShapeDtypeStruct(got.shape, got.dtype)],
        stay, got, now, mom, smem=0,
    )[0]


def put_kernel(replicas, where_ref, stay_ref, got_ref, now_ref, mom_ref, _, __, out_ref, out_mom_ref, outer_ref, moment_ref, sems):
    outer_ref[...], moment_ref[...] = outer_step(replicas, stay_ref, got_ref, now_ref, mom_ref)
    cols = now_ref.shape[1]
    at = pl.ds(pl.multiple_of(where_ref[1] * cols, cols), cols)
    copies = [
        pltpu.make_async_copy(outer_ref, out_ref.at[:, at], sems.at[0]),
        pltpu.make_async_copy(moment_ref, out_mom_ref.at[:, at], sems.at[1]),
    ]
    for copy in copies:
        copy.start()
    for copy in copies:
        copy.wait()


def put_call(replicas, where, stay, got, now, mom, now_copy, mom_copy):
    vmem = pl.BlockSpec(memory_space=pltpu.VMEM)
    anywhere = pl.BlockSpec(memory_space=pl.ANY)
    return pl.pallas_call(
        functools.partial(put_kernel, replicas),
        in_specs=[pl.BlockSpec(memory_space=pltpu.SMEM)] + [vmem] * 4 + [anywhere] * 2,
        out_specs=[anywhere] * 2,
        out_shape=[jax.ShapeDtypeStruct(now_copy.shape, now_copy.dtype)] * 2,
        input_output_aliases={5: 0, 6: 1},
        scratch_shapes=[pltpu.VMEM(now.shape, now.dtype)] * 2 + [pltpu.SemaphoreType.DMA((2,))],
        compiler_params=pltpu.CompilerParams(vmem_limit_bytes=24 * MIB),
        cost_estimate=SMALL,
    )(where, stay, got, now, mom, now_copy, mom_copy)


def place_kernel(offsets, final, factor, where_ref, *refs):
    count = len(offsets)
    msgs = refs[:count]
    acc_ref, _, back_ref, keys_ref, sems = refs[count:]
    toks, keys = acc_ref.shape
    rows = msgs[0].shape[1] - keys
    copies = []
    for i, m in enumerate(offsets):
        start = pl.multiple_of((where_ref[0] ^ m) * rows, rows)
        copy = pltpu.make_async_copy(
            msgs[i].at[:, pl.ds(0, rows)], back_ref.at[:, pl.ds(start, rows)], sems.at[i]
        )
        copy.start()
        copies.append(copy)
    total = acc_ref[...]
    for msg in msgs:
        total = total + msg[:, rows:].astype(jnp.float32)
    if final:
        total = total * factor
    keys_ref[...] = total.astype(keys_ref.dtype)
    for copy in copies:
        copy.wait()


def place_call(where, msgs, acc, back, offsets, final, factor):
    vmem = pl.BlockSpec(memory_space=pltpu.VMEM)
    anywhere = pl.BlockSpec(memory_space=pl.ANY)
    count = len(msgs)
    return pl.pallas_call(
        functools.partial(place_kernel, tuple(offsets), final, factor),
        in_specs=[pl.BlockSpec(memory_space=pltpu.SMEM)] + [vmem] * (count + 1) + [anywhere],
        out_specs=[anywhere, vmem],
        out_shape=[
            jax.ShapeDtypeStruct(back.shape, back.dtype),
            jax.ShapeDtypeStruct(acc.shape, jnp.bfloat16 if final else jnp.float32),
        ],
        input_output_aliases={count + 2: 0},
        scratch_shapes=[pltpu.SemaphoreType.DMA((count,))],
        compiler_params=pltpu.CompilerParams(vmem_limit_bytes=24 * MIB),
        cost_estimate=SMALL,
    )(where, *msgs, acc, back)


def adam_kernel(groups, pieces, factor, where_ref, scal_ref, *refs):
    hids, refs = refs[:groups], refs[groups:]
    cots = [c[...] for c in refs[: groups - 1]]
    weight_ref, first_ref, second_ref = refs[groups - 1 : groups + 2]
    *rest, out_ref = refs[groups + 2 :]
    cots.append(jnp.concatenate([c[...] for c in rest[:pieces]], axis=0))
    grad = part_sum(hids, cots, factor)
    out_ref[...] = adam_step(grad, weight_ref[...], first_ref[...], second_ref[...], scal_ref)


def adam_call(tokens, cot, packs, hid_last, cot_last, weight, first, second, where, scal, factor, frag_cols, part, *base):
    rows, keys = weight.shape
    toks = tokens.shape[0]
    tile = min(1024, rows // 2)
    steps = rows // tile
    lo = part * (steps // 2)
    skip = keys // tile
    groups = len(packs) + 2

    def col(j, w):
        return j + (j >= w[1]).astype(jnp.int32)

    def block(height):
        return pl.BlockSpec((height, frag_cols), lambda i, j, w: (0, col(j, w)))

    state = pl.BlockSpec((tile, frag_cols), lambda i, j, w: (lo + i, col(j, w)))
    return pl.pallas_call(
        functools.partial(adam_kernel, groups, len(cot_last), factor),
        grid_spec=pltpu.PrefetchScalarGridSpec(
            num_scalar_prefetch=1,
            grid=(steps // 2, keys // frag_cols - 1),
            in_specs=[
                pl.BlockSpec(memory_space=pltpu.SMEM),
                pl.BlockSpec((toks, tile), lambda i, j, w: (0, w[0] * steps + lo + i)),
            ]
            + [pl.BlockSpec((toks, tile), lambda i, j, w: (0, skip + lo + i))] * len(packs)
            + [pl.BlockSpec((toks, tile), lambda i, j, w: (0, lo + i))]
            + [block(toks)] * (groups - 1)
            + [state] * 3
            + [block(c.shape[0]) for c in cot_last]
            + [pl.BlockSpec(memory_space=pl.ANY)] * len(base),
            out_specs=state,
        ),
        out_shape=jax.ShapeDtypeStruct((rows, keys), jnp.float32),
        input_output_aliases={4 + 2 * groups + len(cot_last): 0} if base else {},
        compiler_params=pltpu.CompilerParams(vmem_limit_bytes=VMEM),
        cost_estimate=SMALL,
    )(where, scal, tokens, *packs, hid_last, cot, *packs, weight, first, second, *cot_last, *base)


def spread_kernel(bits, where_ref, same_ref, other_ref, base_ref, out_ref, wide_ref, sems):
    chips, size, cols = same_ref.shape
    column = pl.ds(pl.multiple_of(where_ref[1] * cols, cols), cols)
    core = where_ref[2]
    copies = []
    for j in range(chips):
        offset = j ^ where_ref[3]
        at = 0
        for i, k in enumerate(reversed(bits)):
            at = at + (((offset >> k) & 1) << i)
        wide_ref[2 * j + core] = same_ref[at].astype(wide_ref.dtype)
        wide_ref[2 * j + 1 - core] = other_ref[at].astype(wide_ref.dtype)
        for b in (2 * j, 2 * j + 1):
            copy = pltpu.make_async_copy(
                wide_ref.at[b], out_ref.at[pl.ds(b * size, size), column], sems.at[b]
            )
            copy.start()
            copies.append(copy)
    for copy in copies:
        copy.wait()


def spread_call(bits, where, same, other, base):
    chips, size, cols = same.shape
    vmem = pl.BlockSpec(memory_space=pltpu.VMEM)
    anywhere = pl.BlockSpec(memory_space=pl.ANY)
    return pl.pallas_call(
        functools.partial(spread_kernel, bits),
        in_specs=[pl.BlockSpec(memory_space=pltpu.SMEM), vmem, vmem, anywhere],
        out_specs=anywhere,
        out_shape=jax.ShapeDtypeStruct(base.shape, base.dtype),
        input_output_aliases={3: 0},
        scratch_shapes=[
            pltpu.VMEM((2 * chips, size, cols), base.dtype),
            pltpu.SemaphoreType.DMA((2 * chips,)),
        ],
        compiler_params=pltpu.CompilerParams(vmem_limit_bytes=24 * MIB),
        cost_estimate=SMALL,
    )(where, same, other, base)


def per_device(
    hidden,
    key_cotangent,
    local_weight,
    adam_first,
    adam_second,
    outer_weight,
    outer_momentum,
    roster,
    step_count,
):
    tokens = hidden[0]
    cotangent = key_cotangent[0]
    weight = local_weight[0]
    outer_now = outer_weight[0]
    moment_now = outer_momentum[0]
    toks, width = tokens.shape
    rows, keys = weight.shape
    factor = 1.0 / math.sqrt(width)
    frag_cols = keys // FRAGS
    shards = lax.axis_size("fsdp")
    replicas = lax.axis_size("rep")
    shard = lax.axis_index("fsdp")
    replica = lax.axis_index("rep")
    offsets = list(range(1, shards))

    fragment = roster[step_count[0] // FRAGS % ROUNDS, step_count[0] % FRAGS]
    steps_done = (step_count[0] + 1).astype(jnp.float32)
    scale1 = 1.0 / (1.0 - jnp.power(jnp.float32(0.9), steps_done))
    scale2 = 1.0 / (1.0 - jnp.power(jnp.float32(0.95), steps_done))
    scal = jnp.stack([0.9 * scale1, 0.1 * scale1, 0.95 * scale2, 0.05 * scale2])
    chips = replicas // 2
    core, chip = replica % 2, replica // 2
    own_rows = rows // replicas
    where = jnp.stack([shard, fragment, core, chip]).astype(jnp.int32)
    square = shards == 4
    tile = min(512, rows // 4)

    def hid_for(source, m):
        return lax.dynamic_slice_in_dim(source, (shard ^ m) * rows, rows, 1)

    packs = [
        pair(jnp.concatenate([cotangent, hid_for(tokens, m)], axis=1), "fsdp", m)
        for m in offsets[:-1]
    ]

    first, second = adam_first[0], adam_second[0]
    weight_half, back_out, key_acc = own_call(tokens, cotangent, weight, where, factor, tile)
    outer_copy, moment_copy, *outer_frag = copy_call(
        after(where, weight_half), [outer_now, moment_now], frag_cols
    )
    hid_last = hid_for(after(tokens, weight_half), offsets[-1])
    hid_last = pair(after(hid_last, outer_copy, *packs), "fsdp", offsets[-1])
    if square:
        low, high = halves_call(after(packs[0], outer_copy), packs[1], keys)
        packs = [after(x, low, high) for x in packs]
        cot_last = [pair(low, "fsdp", 1), pair(high, "fsdp", 2)]
    else:
        cot_last = [pair(cotangent, "fsdp", offsets[-1])]
    grad_frag, gives = near_call(
        tokens, cotangent, packs, weight_half, after(where, outer_copy), factor, tile, frag_cols
    )
    backs = [pair(x, "fsdp", m) for x, m in zip(gives, offsets)]
    cot_last = [after(c, *gives) for c in cot_last]

    def inner_half(part, hid, *base):
        return adam_call(
            tokens, cotangent, packs, hid, cot_last, weight, first, second, where, scal, factor,
            frag_cols, part, *base,
        )

    keep, give = frag_call(
        hid_last, cot_last, grad_frag, weight, first, second, where, scal, factor, own_rows,
        frag_cols,
    )
    got = pair(give, "rep", 1)
    give_last = last_call(after(hid_last, keep), cot_last, weight_half, factor, tile)
    got = after(got, give_last)
    bits = [k for k in range(chips.bit_length()) if (1 << k) < chips]
    for k in bits:
        keep, leave = split_call(k, where, keep, got)
        got = pair(leave, "rep", 2 << k)
        if k == 0:
            inner = inner_half(0, after(hid_last, leave))
            got = after(got, inner)
    backs.append(pair(give_last, "fsdp", offsets[-1]))
    outer_args = (keep, got, *outer_frag)
    spread = outer_call(replicas, *outer_args)
    for k in reversed(bits):
        got = pair(spread, "rep", 2 << k)
        if k == bits[-1]:
            outer_next, moment_next = put_call(
                replicas, where, after(keep, spread), *outer_args[1:], outer_copy, moment_copy
            )
            back_out, key_acc = place_call(
                where, [after(b, outer_next) for b in backs[:-1]], key_acc, back_out, offsets[:-1],
                False, factor,
            )
            got = after(got, key_acc)
        if k == 0:
            inner = inner_half(1, after(hid_last, spread), inner)
            got = after(got, inner)
        spread = jnp.concatenate([spread, got], axis=0)
    got = pair(spread, "rep", 1)
    new_local = spread_call(bits, where, spread, got, inner)
    back_out, keys_out = place_call(
        where, [after(backs[-1], new_local)], key_acc, back_out, offsets[-1:], True, factor
    )

    return (keys_out[None], back_out[None], new_local[None], outer_next[None], moment_next[None])


def solution(mesh):
    in_specs = (
        P("rep", "fsdp", None),
        P("rep", "fsdp", None),
        P("rep", "fsdp", None),
        P("rep", "fsdp", None),
        P("rep", "fsdp", None),
        P("fsdp", "rep", None),
        P("fsdp", "rep", None),
        P(),
        P(),
    )
    out_specs = (
        P("rep", "fsdp", None),
        P("rep", "fsdp", None),
        P("rep", "fsdp", None),
        P("fsdp", "rep", None),
        P("fsdp", "rep", None),
    )
    return jax.shard_map(
        per_device, mesh=mesh, in_specs=in_specs, out_specs=out_specs, check_vma=False
    )
```

```python
import functools
import math

import jax
import jax.numpy as jnp
from jax import lax
from jax.experimental import pallas as pl
from jax.experimental.pallas import tpu as pltpu
from jax.sharding import PartitionSpec as P

FRAGS = 4
ROUNDS = 8
MIB = 1024 * 1024
VMEM = 48 * MIB
SMALL = pl.CostEstimate(flops=1, bytes_accessed=1, transcendentals=0)


def pair(x, axis, offset):
    size = lax.axis_size(axis)
    return lax.ppermute(x, axis, [(i, i ^ offset) for i in range(size)])


def after(x, *others):
    return lax.optimization_barrier((x, *others))[0]


def row_dot(hid, cot, factor):
    part = lax.dot_general(
        hid, cot, (((0,), (0,)), ((), ())), preferred_element_type=jnp.float32
    )
    return (part * factor).astype(jnp.bfloat16).astype(jnp.float32)


def frag_of_ref(ref, where_ref, like_ref):
    cols = like_ref.shape[-1]
    return ref[:, pl.ds(pl.multiple_of(where_ref[1] * cols, cols), cols)]


def part_sum(hids, cots, factor):
    total = row_dot(hids[0][...], cots[0], factor)
    for hid, cot in zip(hids[1:], cots[1:]):
        total = total + row_dot(hid[...], cot, factor)
    return total


def dot_keys(hid, weight):
    return jnp.dot(hid, weight, preferred_element_type=jnp.float32)


def dot_back(cot, weight, factor):
    out = lax.dot_general(
        cot, weight, (((1,), (1,)), ((), ())), preferred_element_type=jnp.float32
    )
    return (out * factor).astype(jnp.bfloat16)


def add_keys(ref, value):
    @pl.when(pl.program_id(0) == 0)
    def _():
        ref[...] = value

    @pl.when(pl.program_id(0) > 0)
    def _():
        ref[...] += value


def own_kernel(factor, where_ref, tokens_ref, cot_ref, weight_ref, half_ref, back_ref, keys_ref):
    half = weight_ref[...].astype(jnp.bfloat16)
    half_ref[...] = half
    back_ref[...] = dot_back(cot_ref[...], half, factor)
    add_keys(keys_ref, dot_keys(tokens_ref[...], half))


def own_call(tokens, cot, weight, where, factor, tile):
    rows, keys = weight.shape
    toks, width = tokens.shape
    steps = rows // tile
    here = pl.BlockSpec((toks, tile), lambda i, w: (0, w[0] * steps + i))
    block = pl.BlockSpec((tile, keys), lambda i, w: (i, 0))
    whole = pl.BlockSpec((toks, keys), lambda i, w: (0, 0))
    return pl.pallas_call(
        functools.partial(own_kernel, factor),
        grid_spec=pltpu.PrefetchScalarGridSpec(
            num_scalar_prefetch=1,
            grid=(steps,),
            in_specs=[here, whole, block],
            out_specs=[block, here, whole],
        ),
        out_shape=[
            jax.ShapeDtypeStruct((rows, keys), jnp.bfloat16),
            jax.ShapeDtypeStruct((toks, width), jnp.bfloat16),
            jax.ShapeDtypeStruct((toks, keys), jnp.float32),
        ],
        compiler_params=pltpu.CompilerParams(vmem_limit_bytes=VMEM),
        cost_estimate=SMALL,
    )(where, tokens, cot, weight)


def pack(outs, accs, hids, cots, weight, factor, step, steps):
    toks = hids[0].shape[0]
    tile = weight.shape[0]
    rows = tile * steps
    at = pl.ds(pl.multiple_of(step * tile, tile), tile)
    back = dot_back(jnp.concatenate(cots, axis=0), weight, factor)
    part = dot_keys(jnp.concatenate(hids, axis=0), weight)
    for g, (out, acc) in enumerate(zip(outs, accs)):
        mine = slice(g * toks, (g + 1) * toks)
        out[:, at] = back[mine]
        add_keys(acc, part[mine])

    @pl.when(step == steps - 1)
    def _():
        for out, acc in zip(outs, accs):
            out[:, rows:] = acc[...].astype(out.dtype)


def near_kernel(groups, factor, steps, where_ref, *refs):
    hids, cots, weight_ref = refs[:groups], refs[groups : 2 * groups], refs[2 * groups]
    frag_ref, *outs = refs[2 * groups + 1 :]
    frag_ref[...] = part_sum(hids, [frag_of_ref(c, where_ref, frag_ref) for c in cots], factor)
    peers = groups - 1
    pack(
        outs[:peers], outs[peers:], [h[...] for h in hids[1:]], [c[...] for c in cots[1:]],
        weight_ref[...], factor, pl.program_id(0), steps,
    )


def near_call(tokens, cot, packs, weight_half, where, factor, tile, frag_cols):
    rows, keys = weight_half.shape
    toks = tokens.shape[0]
    peers = len(packs)
    groups = peers + 1
    steps = rows // tile
    skip = keys // tile
    block = pl.BlockSpec((tile, keys), lambda i, w: (i, 0))
    whole = pl.BlockSpec((toks, keys), lambda i, w: (0, 0))
    column = pl.BlockSpec((toks, tile), lambda i, w: (0, skip + i))
    out = pl.pallas_call(
        functools.partial(near_kernel, groups, factor, steps),
        grid_spec=pltpu.PrefetchScalarGridSpec(
            num_scalar_prefetch=1,
            grid=(steps,),
            in_specs=[pl.BlockSpec((toks, tile), lambda i, w: (0, w[0] * steps + i))]
            + [column] * peers
            + [whole] * groups
            + [block],
            out_specs=[pl.BlockSpec((tile, frag_cols), lambda i, w: (i, w[1]))]
            + [pl.BlockSpec((toks, rows + keys), lambda i, w: (0, 0))] * peers,
            scratch_shapes=[pltpu.VMEM((toks, keys), jnp.float32)] * peers,
        ),
        out_shape=[jax.ShapeDtypeStruct((rows, keys), jnp.float32)]
        + [jax.ShapeDtypeStruct((toks, rows + keys), jnp.bfloat16)] * peers,
        compiler_params=pltpu.CompilerParams(vmem_limit_bytes=VMEM),
        cost_estimate=SMALL,
    )(where, tokens, *packs, cot, *packs, weight_half)
    return out[0], list(out[1:])


def last_kernel(factor, steps, hid_ref, weight_ref, *refs):
    *cots, out_ref, acc_ref = refs
    cot = jnp.concatenate([c[...] for c in cots], axis=0)
    pack(
        [out_ref], [acc_ref], [hid_ref[...]], [cot], weight_ref[...], factor, pl.program_id(0), steps
    )


def last_call(hid, cots, weight_half, factor, tile):
    rows, keys = weight_half.shape
    toks = hid.shape[0]
    steps = rows // tile
    return pl.pallas_call(
        functools.partial(last_kernel, factor, steps),
        grid=(steps,),
        in_specs=[
            pl.BlockSpec((toks, tile), lambda i: (0, i)),
            pl.BlockSpec((tile, keys), lambda i: (i, 0)),
        ]
        + [pl.BlockSpec(c.shape, lambda i: (0, 0)) for c in cots],
        out_specs=pl.BlockSpec((toks, rows + keys), lambda i: (0, 0)),
        out_shape=jax.ShapeDtypeStruct((toks, rows + keys), jnp.bfloat16),
        scratch_shapes=[pltpu.VMEM((toks, keys), jnp.float32)],
        compiler_params=pltpu.CompilerParams(vmem_limit_bytes=32 * MIB),
        cost_estimate=SMALL,
    )(hid, weight_half, *cots)


def adam_step(grad, weight, first, second, scal_ref):
    first = scal_ref[0] * first + scal_ref[1] * grad
    second = scal_ref[2] * second + scal_ref[3] * (grad * grad)
    return 0.99 * weight - 0.1 * (first / (jnp.sqrt(second) + 1e-08))


def frag_kernel(factor, where_ref, scal_ref, hid_ref, *refs):
    *cots, grad_ref, weight_ref, first_ref, second_ref, keep_ref, give_ref, here_ref, sems = refs
    chips, size = keep_ref.shape[:2]
    cols = keep_ref.shape[2]
    even_mine = where_ref[2] == 0
    column = pl.ds(pl.multiple_of(where_ref[1] * cols, cols), cols)
    copies = []
    for j in range(chips):
        at = pl.ds(2 * j * size, 2 * size)
        sources = [x.at[at, column] for x in (grad_ref, weight_ref, first_ref, second_ref)]
        copies.append(
            [
                pltpu.make_async_copy(source, here_ref.at[i, at, :], sems.at[i, j])
                for i, source in enumerate(sources)
            ]
        )
        for copy in copies[-1]:
            copy.start()
    cot = jnp.concatenate([c[:, column] for c in cots], axis=0)
    for j in range(chips):
        at = pl.ds(2 * j * size, 2 * size)
        part = row_dot(hid_ref[:, at], cot, factor)
        for copy in copies[j]:
            copy.wait()
        inner = adam_step(
            here_ref[0, at, :] + part, here_ref[1, at, :], here_ref[2, at, :], here_ref[3, at, :],
            scal_ref,
        )
        even, odd = inner[:size], inner[size:]
        keep_ref[j] = jnp.where(even_mine, even, odd).astype(keep_ref.dtype)
        give_ref[j] = jnp.where(even_mine, odd, even).astype(give_ref.dtype)


def local_call(kernel, outs, *args, smem=1, limit=24):
    vmem = pl.BlockSpec(memory_space=pltpu.VMEM)
    return pl.pallas_call(
        kernel,
        in_specs=[pl.BlockSpec(memory_space=pltpu.SMEM)] * smem + [vmem] * (len(args) - smem),
        out_specs=[vmem] * len(outs),
        out_shape=outs,
        compiler_params=pltpu.CompilerParams(vmem_limit_bytes=limit * MIB),
        cost_estimate=SMALL,
    )(*args)


def frag_call(hid, cots, grad, weight, first, second, where, scal, factor, own_rows, cols):
    rows = grad.shape[0]
    chips = rows // (2 * own_rows)
    vmem = pl.BlockSpec(memory_space=pltpu.VMEM)
    out = jax.ShapeDtypeStruct((chips, own_rows, cols), jnp.bfloat16)
    return pl.pallas_call(
        functools.partial(frag_kernel, factor),
        in_specs=[pl.BlockSpec(memory_space=pltpu.SMEM)] * 2
        + [vmem] * (1 + len(cots))
        + [pl.BlockSpec(memory_space=pl.ANY)] * 4,
        out_specs=[vmem, vmem],
        out_shape=[out, out],
        scratch_shapes=[
            pltpu.VMEM((4, rows, cols), jnp.float32), pltpu.SemaphoreType.DMA((4, chips))
        ],
        compiler_params=pltpu.CompilerParams(vmem_limit_bytes=VMEM),
        cost_estimate=SMALL,
    )(where, scal, hid, *cots, grad, weight, first, second)


def split_kernel(bit, where_ref, mine_ref, got_ref, stay_ref, leave_ref):
    low = ((where_ref[3] >> bit) & 1) == 0
    for i in range(stay_ref.shape[0]):
        sums = [
            mine_ref[j].astype(jnp.float32) + got_ref[j].astype(jnp.float32)
            for j in (2 * i, 2 * i + 1)
        ]
        stay_ref[i] = jnp.where(low, sums[0], sums[1])
        leave_ref[i] = jnp.where(low, sums[1], sums[0]).astype(leave_ref.dtype)


def split_call(bit, where, mine, got):
    shape = (mine.shape[0] // 2,) + mine.shape[1:]
    return local_call(
        functools.partial(split_kernel, bit),
        [jax.ShapeDtypeStruct(shape, jnp.float32), jax.ShapeDtypeStruct(shape, jnp.bfloat16)],
        where, mine, got,
    )


def halves_kernel(x_ref, y_ref, low_ref, high_ref):
    low_ref[...] = y_ref[...]
    high_ref[...] = x_ref[...]


def halves_call(pack_x, pack_y, keys):
    half = pack_x.shape[0] // 2
    first = pl.BlockSpec((half, keys), lambda i: (0, 0))
    second = pl.BlockSpec((half, keys), lambda i: (1, 0))
    return pl.pallas_call(
        halves_kernel,
        grid=(1,),
        in_specs=[second, first],
        out_specs=[first, first],
        out_shape=[jax.ShapeDtypeStruct((half, keys), pack_x.dtype)] * 2,
        cost_estimate=SMALL,
    )(pack_x, pack_y)


def copy_kernel(count, where_ref, *refs):
    for i in range(count):
        refs[count + i][...] = refs[i][...]
        refs[2 * count + i][...] = frag_of_ref(refs[i], where_ref, refs[2 * count + i])


def copy_call(where, arrays, frag_cols):
    count = len(arrays)
    rows, cols = arrays[0].shape
    block = pl.BlockSpec((rows // 2, cols), lambda i, w: (i, 0))
    part = pl.BlockSpec((rows // 2, frag_cols), lambda i, w: (i, 0))
    return pl.pallas_call(
        functools.partial(copy_kernel, count),
        grid_spec=pltpu.PrefetchScalarGridSpec(
            num_scalar_prefetch=1,
            grid=(2,),
            in_specs=[block] * count,
            out_specs=[block] * count + [part] * count,
        ),
        out_shape=[jax.ShapeDtypeStruct(x.shape, x.dtype) for x in arrays]
        + [jax.ShapeDtypeStruct((rows, frag_cols), x.dtype) for x in arrays],
        compiler_params=pltpu.CompilerParams(vmem_limit_bytes=VMEM),
        cost_estimate=SMALL,
    )(where, *arrays)


def outer_step(replicas, stay_ref, got_ref, now_ref, mom_ref):
    total = stay_ref[0] + got_ref[0].astype(jnp.float32)
    pseudo = now_ref[...] - total / replicas
    moment = 0.9 * mom_ref[...] + pseudo
    return now_ref[...] - 0.7 * (pseudo + 0.9 * moment), moment


def outer_kernel(replicas, *refs):
    spread_ref = refs[-1]
    spread_ref[0] = outer_step(replicas, *refs[:-1])[0].astype(spread_ref.dtype)


def outer_call(replicas, stay, got, now, mom):
    return local_call(
        functools.partial(outer_kernel, replicas),
        [jax.ShapeDtypeStruct(got.shape, got.dtype)],
        stay, got, now, mom, smem=0,
    )[0]


def put_kernel(replicas, where_ref, stay_ref, got_ref, now_ref, mom_ref, _, __, out_ref, out_mom_ref, outer_ref, moment_ref, sems):
    outer_ref[...], moment_ref[...] = outer_step(replicas, stay_ref, got_ref, now_ref, mom_ref)
    cols = now_ref.shape[1]
    at = pl.ds(pl.multiple_of(where_ref[1] * cols, cols), cols)
    copies = [
        pltpu.make_async_copy(outer_ref, out_ref.at[:, at], sems.at[0]),
        pltpu.make_async_copy(moment_ref, out_mom_ref.at[:, at], sems.at[1]),
    ]
    for copy in copies:
        copy.start()
    for copy in copies:
        copy.wait()


def put_call(replicas, where, stay, got, now, mom, now_copy, mom_copy):
    vmem = pl.BlockSpec(memory_space=pltpu.VMEM)
    anywhere = pl.BlockSpec(memory_space=pl.ANY)
    return pl.pallas_call(
        functools.partial(put_kernel, replicas),
        in_specs=[pl.BlockSpec(memory_space=pltpu.SMEM)] + [vmem] * 4 + [anywhere] * 2,
        out_specs=[anywhere] * 2,
        out_shape=[jax.ShapeDtypeStruct(now_copy.shape, now_copy.dtype)] * 2,
        input_output_aliases={5: 0, 6: 1},
        scratch_shapes=[pltpu.VMEM(now.shape, now.dtype)] * 2 + [pltpu.SemaphoreType.DMA((2,))],
        compiler_params=pltpu.CompilerParams(vmem_limit_bytes=24 * MIB),
        cost_estimate=SMALL,
    )(where, stay, got, now, mom, now_copy, mom_copy)


def place_kernel(offsets, final, factor, where_ref, *refs):
    count = len(offsets)
    msgs = refs[:count]
    acc_ref, _, back_ref, keys_ref, sems = refs[count:]
    toks, keys = acc_ref.shape
    rows = msgs[0].shape[1] - keys
    copies = []
    for i, m in enumerate(offsets):
        start = pl.multiple_of((where_ref[0] ^ m) * rows, rows)
        copy = pltpu.make_async_copy(
            msgs[i].at[:, pl.ds(0, rows)], back_ref.at[:, pl.ds(start, rows)], sems.at[i]
        )
        copy.start()
        copies.append(copy)
    total = acc_ref[...]
    for msg in msgs:
        total = total + msg[:, rows:].astype(jnp.float32)
    if final:
        total = total * factor
    keys_ref[...] = total.astype(keys_ref.dtype)
    for copy in copies:
        copy.wait()


def place_call(where, msgs, acc, back, offsets, final, factor):
    vmem = pl.BlockSpec(memory_space=pltpu.VMEM)
    anywhere = pl.BlockSpec(memory_space=pl.ANY)
    count = len(msgs)
    return pl.pallas_call(
        functools.partial(place_kernel, tuple(offsets), final, factor),
        in_specs=[pl.BlockSpec(memory_space=pltpu.SMEM)] + [vmem] * (count + 1) + [anywhere],
        out_specs=[anywhere, vmem],
        out_shape=[
            jax.ShapeDtypeStruct(back.shape, back.dtype),
            jax.ShapeDtypeStruct(acc.shape, jnp.bfloat16 if final else jnp.float32),
        ],
        input_output_aliases={count + 2: 0},
        scratch_shapes=[pltpu.SemaphoreType.DMA((count,))],
        compiler_params=pltpu.CompilerParams(vmem_limit_bytes=24 * MIB),
        cost_estimate=SMALL,
    )(where, *msgs, acc, back)


def adam_kernel(groups, pieces, factor, where_ref, scal_ref, *refs):
    hids, refs = refs[:groups], refs[groups:]
    cots = [c[...] for c in refs[: groups - 1]]
    weight_ref, first_ref, second_ref = refs[groups - 1 : groups + 2]
    *rest, out_ref = refs[groups + 2 :]
    cots.append(jnp.concatenate([c[...] for c in rest[:pieces]], axis=0))
    grad = part_sum(hids, cots, factor)
    out_ref[...] = adam_step(grad, weight_ref[...], first_ref[...], second_ref[...], scal_ref)


def adam_call(tokens, cot, packs, hid_last, cot_last, weight, first, second, where, scal, factor, frag_cols, j, *base):
    rows, keys = weight.shape
    toks = tokens.shape[0]
    tile = min(1024, rows // 2)
    steps = rows // tile
    skip = keys // tile
    groups = len(packs) + 2

    def col(w):
        return j + (w[1] <= j).astype(jnp.int32)

    def block(height):
        return pl.BlockSpec((height, frag_cols), lambda i, w: (0, col(w)))

    state = pl.BlockSpec((tile, frag_cols), lambda i, w: (i, col(w)))
    return pl.pallas_call(
        functools.partial(adam_kernel, groups, len(cot_last), factor),
        grid_spec=pltpu.PrefetchScalarGridSpec(
            num_scalar_prefetch=1,
            grid=(steps,),
            in_specs=[
                pl.BlockSpec(memory_space=pltpu.SMEM),
                pl.BlockSpec((toks, tile), lambda i, w: (0, w[0] * steps + i)),
            ]
            + [pl.BlockSpec((toks, tile), lambda i, w: (0, skip + i))] * len(packs)
            + [pl.BlockSpec((toks, tile), lambda i, w: (0, i))]
            + [block(toks)] * (groups - 1)
            + [state] * 3
            + [block(c.shape[0]) for c in cot_last]
            + [pl.BlockSpec(memory_space=pl.ANY)] * len(base),
            out_specs=state,
        ),
        out_shape=jax.ShapeDtypeStruct((rows, keys), jnp.float32),
        input_output_aliases={4 + 2 * groups + len(cot_last): 0} if base else {},
        compiler_params=pltpu.CompilerParams(vmem_limit_bytes=VMEM),
        cost_estimate=SMALL,
    )(where, scal, tokens, *packs, hid_last, cot, *packs, weight, first, second, *cot_last, *base)


def spread_kernel(bits, where_ref, same_ref, other_ref, base_ref, out_ref, wide_ref, sems):
    chips, size, cols = same_ref.shape
    column = pl.ds(pl.multiple_of(where_ref[1] * cols, cols), cols)
    core = where_ref[2]
    copies = []
    for j in range(chips):
        offset = j ^ where_ref[3]
        at = 0
        for i, k in enumerate(reversed(bits)):
            at = at + (((offset >> k) & 1) << i)
        wide_ref[2 * j + core] = same_ref[at].astype(wide_ref.dtype)
        wide_ref[2 * j + 1 - core] = other_ref[at].astype(wide_ref.dtype)
        for b in (2 * j, 2 * j + 1):
            copy = pltpu.make_async_copy(
                wide_ref.at[b], out_ref.at[pl.ds(b * size, size), column], sems.at[b]
            )
            copy.start()
            copies.append(copy)
    for copy in copies:
        copy.wait()


def spread_call(bits, where, same, other, base):
    chips, size, cols = same.shape
    vmem = pl.BlockSpec(memory_space=pltpu.VMEM)
    anywhere = pl.BlockSpec(memory_space=pl.ANY)
    return pl.pallas_call(
        functools.partial(spread_kernel, bits),
        in_specs=[pl.BlockSpec(memory_space=pltpu.SMEM), vmem, vmem, anywhere],
        out_specs=anywhere,
        out_shape=jax.ShapeDtypeStruct(base.shape, base.dtype),
        input_output_aliases={3: 0},
        scratch_shapes=[
            pltpu.VMEM((2 * chips, size, cols), base.dtype),
            pltpu.SemaphoreType.DMA((2 * chips,)),
        ],
        compiler_params=pltpu.CompilerParams(vmem_limit_bytes=24 * MIB),
        cost_estimate=SMALL,
    )(where, same, other, base)


def per_device(
    hidden,
    key_cotangent,
    local_weight,
    adam_first,
    adam_second,
    outer_weight,
    outer_momentum,
    roster,
    step_count,
):
    tokens = hidden[0]
    cotangent = key_cotangent[0]
    weight = local_weight[0]
    outer_now = outer_weight[0]
    moment_now = outer_momentum[0]
    toks, width = tokens.shape
    rows, keys = weight.shape
    factor = 1.0 / math.sqrt(width)
    frag_cols = keys // FRAGS
    shards = lax.axis_size("fsdp")
    replicas = lax.axis_size("rep")
    shard = lax.axis_index("fsdp")
    replica = lax.axis_index("rep")
    offsets = list(range(1, shards))

    fragment = roster[step_count[0] // FRAGS % ROUNDS, step_count[0] % FRAGS]
    steps_done = (step_count[0] + 1).astype(jnp.float32)
    scale1 = 1.0 / (1.0 - jnp.power(jnp.float32(0.9), steps_done))
    scale2 = 1.0 / (1.0 - jnp.power(jnp.float32(0.95), steps_done))
    scal = jnp.stack([0.9 * scale1, 0.1 * scale1, 0.95 * scale2, 0.05 * scale2])
    chips = replicas // 2
    core, chip = replica % 2, replica // 2
    own_rows = rows // replicas
    where = jnp.stack([shard, fragment, core, chip]).astype(jnp.int32)
    square = shards == 4
    tile = min(512, rows // 4)

    def hid_for(source, m):
        return lax.dynamic_slice_in_dim(source, (shard ^ m) * rows, rows, 1)

    packs = [
        pair(jnp.concatenate([cotangent, hid_for(tokens, m)], axis=1), "fsdp", m)
        for m in offsets[:-1]
    ]

    first, second = adam_first[0], adam_second[0]
    weight_half, back_out, key_acc = own_call(tokens, cotangent, weight, where, factor, tile)
    outer_copy, moment_copy, *outer_frag = copy_call(
        after(where, weight_half), [outer_now, moment_now], frag_cols
    )
    hid_last = hid_for(after(tokens, weight_half), offsets[-1])
    hid_last = pair(after(hid_last, outer_copy, *packs), "fsdp", offsets[-1])
    if square:
        low, high = halves_call(after(packs[0], outer_copy), packs[1], keys)
        packs = [after(x, low, high) for x in packs]
        cot_last = [pair(low, "fsdp", 1), pair(high, "fsdp", 2)]
    else:
        cot_last = [pair(cotangent, "fsdp", offsets[-1])]
    grad_frag, gives = near_call(
        tokens, cotangent, packs, weight_half, after(where, outer_copy), factor, tile, frag_cols
    )
    backs = [pair(x, "fsdp", m) for x, m in zip(gives, offsets)]
    cot_last = [after(c, *gives) for c in cot_last]

    inner = []

    def inner_step(blocks, *ready):
        for _ in range(blocks):
            if len(inner) < FRAGS - 1:
                hid = after(hid_last, *ready)
                inner.append(
                    adam_call(
                        tokens, cotangent, packs, hid, cot_last, weight, first, second, where, scal,
                        factor, frag_cols, len(inner), *inner[-1:],
                    )
                )
        return inner[-1]

    keep, give = frag_call(
        hid_last, cot_last, grad_frag, weight, first, second, where, scal, factor, own_rows,
        frag_cols,
    )
    got = pair(give, "rep", 1)
    give_last = last_call(after(hid_last, keep), cot_last, weight_half, factor, tile)
    got = after(got, give_last)
    bits = [k for k in range(chips.bit_length()) if (1 << k) < chips]
    for k in bits:
        keep, leave = split_call(k, where, keep, got)
        got = pair(leave, "rep", 2 << k)
        if k in (0, bits[-1]):
            got = after(got, inner_step(1, leave))
    backs.append(pair(give_last, "fsdp", offsets[-1]))
    outer_args = (keep, got, *outer_frag)
    spread = outer_call(replicas, *outer_args)
    for k in reversed(bits):
        got = pair(spread, "rep", 2 << k)
        if k == bits[-1]:
            outer_next, moment_next = put_call(
                replicas, where, after(keep, spread), *outer_args[1:], outer_copy, moment_copy
            )
            back_out, key_acc = place_call(
                where, [after(b, outer_next) for b in backs[:-1]], key_acc, back_out, offsets[:-1],
                False, factor,
            )
            got = after(got, key_acc)
        if k == 0:
            got = after(got, inner_step(FRAGS, spread))
        spread = jnp.concatenate([spread, got], axis=0)
    got = pair(spread, "rep", 1)
    new_local = spread_call(bits, where, spread, got, inner[-1])
    back_out, keys_out = place_call(
        where, [after(backs[-1], new_local)], key_acc, back_out, offsets[-1:], True, factor
    )

    return (keys_out[None], back_out[None], new_local[None], outer_next[None], moment_next[None])


def solution(mesh):
    in_specs = (
        P("rep", "fsdp", None),
        P("rep", "fsdp", None),
        P("rep", "fsdp", None),
        P("rep", "fsdp", None),
        P("rep", "fsdp", None),
        P("fsdp", "rep", None),
        P("fsdp", "rep", None),
        P(),
        P(),
    )
    out_specs = (
        P("rep", "fsdp", None),
        P("rep", "fsdp", None),
        P("rep", "fsdp", None),
        P("fsdp", "rep", None),
        P("fsdp", "rep", None),
    )
    return jax.shard_map(
        per_device, mesh=mesh, in_specs=in_specs, out_specs=out_specs, check_vma=False
    )
```
